256 devices in a mesh: ctx: 16 (over z, core), head: 16 (over x, y).
Axes of the slice: x: 4, y: 4, z: 8, core: 2. Of those that a mesh axis runs over, the one named last changes fastest.
Arguments:
- tokens: bfloat16 [32768, 16384], P(('ctx', 'head')), may hold values from -6 to 6
- b_proj: bfloat16 [32768, 2048], P(('ctx', 'head')), may hold values from -0.375 to 0.375
- c_proj: bfloat16 [32768, 2048], P(('ctx', 'head')), may hold values from -0.119628906 to 0.119628906
- log_decay: bfloat16 [32768, 256], P(('ctx', 'head')), may hold values from -2 to 0, as said below
- bypass_gain_vector: float32 [256], P('head'), may hold values from 0.5 to 1.5
Outputs:
- mixed: bfloat16 [32768, 16384], P(('ctx', 'head'))
The draws below stay inside these ranges and needn't reach their ends.
Inputs may be any that keep to these rules, and one draw needn't show every extreme that they name: `log_decay`: non-positive log decays.
All inputs are finite; a program needn't handle non-finite values.
Results may differ from the reference program's by a relative error of at most 0.014.
Values may be sent and summed in bfloat16 or wider, within the bound.
No kernel may reach another device: no remote copies, remote signals or barrier semaphores. Data moves between devices by JAX's collectives and lax.ppermute only.
A program may use at most 192 MiB of HBM per device.

```python
import math
import jax
import jax.numpy as jnp
from jax import lax

H = 256
P_SIZE = 64
N = 256
G = 8
Q = 256
L_CTX = 2048
STREAM_LENGTH = 32768


def draw_log_decay(key, part):
    key = jax.random.fold_in(key, 7)
    randomness_seeds = jax.random.split(key, 8)
    slow_share = 0.5
    shard_count = STREAM_LENGTH // L_CTX
    slow_head = jax.random.uniform(randomness_seeds[0], (H,)) < slow_share
    fast_rate = jnp.exp(jax.random.uniform(randomness_seeds[1], (H,), minval=math.log(1.0 / 400.0), maxval=math.log(1.0 / 30.0)))
    slow_rate = jnp.exp(jax.random.uniform(randomness_seeds[2], (H,), minval=math.log(0.1), maxval=math.log(0.3))) / STREAM_LENGTH
    fast_turn = jax.random.uniform(randomness_seeds[7], (shard_count, H)) < 0.5
    fast_mode = jnp.logical_and(jnp.logical_not(slow_head)[None, :], fast_turn)
    shard_rate = jnp.where(fast_mode, fast_rate[None, :], slow_rate[None, :])
    shard_factor = jnp.exp(jax.random.uniform(randomness_seeds[4], (shard_count, H), minval=math.log(0.5), maxval=math.log(2.0)))
    token_rate = jnp.repeat(shard_rate * shard_factor, L_CTX, axis=0, total_repeat_length=STREAM_LENGTH)
    jitter_shift_amount = jnp.exp(jax.random.uniform(randomness_seeds[3], (STREAM_LENGTH, H), minval=math.log(0.5), maxval=math.log(2.0)))
    spike_locations = jax.random.randint(randomness_seeds[5], (2,), 0, STREAM_LENGTH)
    spike_duration = jnp.log(jax.random.uniform(randomness_seeds[6], (2,), minval=0.5, maxval=0.8))
    appearance_index = jnp.arange(STREAM_LENGTH)[:, None] == spike_locations[None, :]
    spike_indicator = jnp.sum(jnp.where(appearance_index, spike_duration[None, :], 0.0), axis=1)
    carried_values = -token_rate * jitter_shift_amount + spike_indicator[:, None]
    return carried_values.astype(jnp.float32).astype(jnp.bfloat16)


def level_of(own_key, dims, pieces, least, largest):
    def one(dim, parts):
        draws = jax.random.uniform(jax.random.fold_in(jax.random.fold_in(own_key, 6), dim), (parts,), jnp.float32, least / len(pieces), largest / len(pieces))
        return jnp.repeat(jnp.exp(draws), dims[dim] // parts).reshape((-1,) + (1,) * (len(dims) - dim - 1))

    factor_of = one(*pieces[0])
    for cut in pieces[1:]:
        factor_of = factor_of * one(*cut)
    return factor_of


def normal_values(rng, shape, scale, reach, cuts=(), held_as=jnp.bfloat16):
    array = scale * jax.random.normal(rng, shape, jnp.float32)
    if cuts:
        array = array * level_of(rng, shape, cuts, -0.22, 0.18)
    return jnp.clip(array, -reach, reach).astype(held_as)


def setup_inputs(seed: int = 0) -> dict:
    keys = jax.random.split(jax.random.key(seed), 6)
    tokens = normal_values(keys[0], (STREAM_LENGTH, H * P_SIZE), 1.0, 6.0, ((0, 256),))
    b_proj = normal_values(keys[1], (STREAM_LENGTH, G * N), N ** -0.5, 0.375, ((0, 256),))
    c_proj = normal_values(keys[2], (STREAM_LENGTH, G * N), 0.02, 0.119628906, ((0, 256),))
    log_decay = draw_log_decay(jax.random.fold_in(keys[5], 71), 0)
    bypass_gain_vector = jnp.clip(0.5 + 1.0 * jax.random.uniform(keys[4], (H,), jnp.float32) ** level_of(keys[4], (H,), ((0, 16),), -0.2, 0.2), 0.5, 1.5)
    return dict(tokens=tokens, b_proj=b_proj, c_proj=c_proj, log_decay=log_decay, bypass_gain_vector=bypass_gain_vector)


def reference(tokens, b_proj, c_proj, log_decay, bypass_gain_vector):
    block_list = STREAM_LENGTH // Q
    per_group = H // G
    values = tokens.reshape(block_list, Q, G, per_group, P_SIZE)
    b_rows = b_proj.reshape(block_list, Q, G, N)
    c_rows = c_proj.reshape(block_list, Q, G, N)
    rates = log_decay.astype(jnp.float32).reshape(block_list, Q, G, per_group)
    gains = bypass_gain_vector.reshape(G, per_group)
    forward_only_masking = jnp.arange(Q)[:, None] >= jnp.arange(Q)[None, :]

    def advance(carry, item):
        value_blk, b_blk, c_blk, rate_blk = item
        cumul = jnp.cumsum(rate_blk, axis=0)
        scores = jnp.einsum("qgn,kgn->gqk", c_blk.astype(jnp.float32), b_blk.astype(jnp.float32))
        moved = jnp.moveaxis(cumul, 0, -1)
        spread = moved[..., :, None] - moved[..., None, :]
        decays = jnp.exp(jnp.where(forward_only_masking, spread, -jnp.inf))
        weights = (scores[:, None] * decays).astype(jnp.bfloat16)
        weights = lax.optimization_barrier(weights).astype(jnp.float32)
        inner = jnp.einsum("ghqk,kghp->qghp", weights, value_blk.astype(jnp.float32))
        rounded = lax.optimization_barrier(carry.astype(jnp.bfloat16)).astype(jnp.float32)
        outer = jnp.einsum("qgn,ghpn->qghp", c_blk.astype(jnp.float32), rounded) * jnp.exp(cumul)[..., None]
        tail = jnp.exp(cumul[-1][None] - cumul)
        b_weighted = (b_blk[:, :, None, :].astype(jnp.float32) * tail[..., None]).astype(jnp.bfloat16)
        b_weighted = lax.optimization_barrier(b_weighted).astype(jnp.float32)
        block_state = jnp.einsum("kghn,kghp->ghpn", b_weighted, value_blk.astype(jnp.float32))
        new_state = jnp.exp(cumul[-1])[..., None, None] * carry + block_state
        result = inner + outer + gains[None, :, :, None] * value_blk.astype(jnp.float32)
        return new_state, result.astype(jnp.bfloat16)

    initial = jnp.zeros((G, per_group, P_SIZE, N), jnp.float32)
    _, outputs = lax.scan(advance, initial, (values, b_rows, c_rows, rates))
    return outputs.reshape(STREAM_LENGTH, H * P_SIZE)
```

```python
import functools

import jax
import jax.numpy as jnp
from jax import lax
from jax.experimental import pallas as pl
from jax.experimental.pallas import tpu as pltpu
from jax.sharding import PartitionSpec as P

P_SIZE = 64
N = 256
Q = 256
SUB = 64
PARTS = 2
ROWS = 128
HALF = ROWS // 2
HEADS = 16
SLABS = 4
LANES = 128
PIECES = 16
LOG2E = 1.4426950408889634
F32 = jnp.float32
BF16 = jnp.bfloat16
VMEM_LIMIT = 60 * 1024 * 1024


def dot(a, b, dims):
    return lax.dot_general(a, b, (dims, ((), ())), preferred_element_type=F32)


def call(kernel, name, cost, limit=VMEM_LIMIT, **kwargs):
    flops, mib, exps = cost
    return pl.pallas_call(
        kernel,
        name=name,
        compiler_params=pltpu.CompilerParams(vmem_limit_bytes=limit),
        cost_estimate=pl.CostEstimate(
            flops=flops, bytes_accessed=mib * 2**20, transcendentals=exps
        ),
        **kwargs,
    )


def pack_kernel(x_ref, b_ref, c_ref, d_ref, first_ref, second_ref):
    width = second_ref.shape[2]
    turned = jnp.transpose(d_ref[...].astype(F32)).astype(BF16)
    turned = jnp.where(pl.program_id(0) % 2 == 0, turned[: 4 * HEADS], turned[4 * HEADS :])
    for k in range(second_ref.shape[0]):
        cols = slice((k // 2) * N, (k // 2 + 1) * N)
        for part, (out_ref, ref) in enumerate(((first_ref, b_ref), (second_ref, c_ref))):
            at = (PARTS * k + part) * width
            out_ref[k, :ROWS] = x_ref[:, at : at + width]
            out_ref[k, ROWS : ROWS + HALF, :N] = ref[:HALF, cols]
            out_ref[k, ROWS : ROWS + HALF, N:] = ref[HALF:, cols]
        first_ref[k, ROWS + HALF :, :ROWS] = turned[k * HEADS : (k + 1) * HEADS]
        first_ref[k, ROWS + HALF :, ROWS:] = jnp.zeros((HEADS, width - ROWS), BF16)


def pack(tokens, b_proj, c_proj, log_decay, n_head):
    cols = tokens.shape[1]
    width = cols // n_head // PARTS
    heights = (ROWS + HALF + HEADS, ROWS + HALF)
    return call(
        pack_kernel,
        "pack",
        (0, 12, 0),
        grid=(n_head // 4,),
        in_specs=[
            pl.BlockSpec((ROWS, 4 * PARTS * width), lambda i: (0, i)),
            pl.BlockSpec((ROWS, 2 * N), lambda i: (0, i)),
            pl.BlockSpec((ROWS, 2 * N), lambda i: (0, i)),
            pl.BlockSpec((ROWS, ROWS), lambda i: (0, i // 2)),
        ],
        out_specs=[pl.BlockSpec((4, height, width), lambda i: (i, 0, 0)) for height in heights],
        out_shape=[jax.ShapeDtypeStruct((n_head, height, width), BF16) for height in heights],
    )(tokens, b_proj, c_proj, log_decay)


def folded(ref):
    pieces = []
    for k in range(ref.shape[0]):
        pieces += [ref[k, :, :N], ref[k, :, N:]]
    return jnp.concatenate(pieces, axis=0)


def rows_of(ref):
    return jnp.concatenate([ref[k] for k in range(ref.shape[0])], axis=0)


def three(whole):
    high = whole.astype(BF16).astype(F32)
    mid = (whole - high).astype(BF16).astype(F32)
    return high, mid, whole - high - mid


def in_pieces(whole):
    high, mid, low = three(whole)
    row = lax.broadcasted_iota(jnp.int32, (PIECES, whole.shape[1]), 0)
    out = jnp.where(row == 0, high, jnp.where(row == 1, mid, jnp.where(row == 2, low, 0.0)))
    return out.astype(BF16)


def of_pieces(rows):
    return jnp.sum(rows.astype(F32), axis=0, keepdims=True)


def block_sums(d_ref, block):
    turned = jnp.concatenate([d_ref[2 * block], d_ref[2 * block + 1]], axis=1)
    u = lax.broadcasted_iota(jnp.int32, (Q, Q), 0)
    t = lax.broadcasted_iota(jnp.int32, (Q, Q), 1)
    upper = (u <= t).astype(F32).astype(BF16)
    sums = dot(turned, upper, ((1,), (0,))) * LOG2E
    rest = jnp.zeros((LANES - 3 * HEADS, Q), F32)
    return jnp.transpose(jnp.concatenate([*three(sums), rest], axis=0)).astype(BF16)


def spread_sums(part, pieces, width):
    row = lax.broadcasted_iota(jnp.int32, (LANES, width), 0)
    col = lax.broadcasted_iota(jnp.int32, (LANES, width), 1)
    head = col // P_SIZE + part * (HEADS // PARTS)
    taken = jnp.logical_and(row % HEADS == head, row < 3 * HEADS)
    return dot(pieces, taken.astype(F32).astype(BF16), ((1,), (0,)))


def step_of(i, shift):
    return jnp.maximum(i - shift, 0)


def x_spec(width, shift=0):
    return pl.BlockSpec((SLABS, ROWS, width), lambda i: (step_of(i, shift), 0, 0))


def bc_spec(width, shift=0):
    return pl.BlockSpec((SLABS, HALF, width), lambda i: (step_of(i, shift), ROWS // HALF, 0))


def flat_spec(width, shift=0):
    return pl.BlockSpec((SLABS * ROWS, width), lambda i: (step_of(i, shift), 0))


def smem_spec():
    return pl.BlockSpec(memory_space=pltpu.SMEM)


BLOCKS = SLABS * ROWS // Q


def states_kernel(part, *refs):
    if part == 0:
        x_ref, b_ref, d_ref, end_ref, sums_ref, state, total = refs
    else:
        x_ref, b_ref, sums_ref, end_ref, state, total = refs
    step = pl.program_id(0)
    width = x_ref.shape[2]

    @pl.when(step == 0)
    def _():
        state[...] = jnp.zeros_like(state)
        total[...] = jnp.zeros_like(total)

    if part == 0:
        pieces = jnp.concatenate([block_sums(d_ref, k) for k in range(BLOCKS)], axis=0)
        sums_ref[...] = pieces
    else:
        pieces = sums_ref[...]
    s = spread_sums(part, pieces, width)
    later = jnp.zeros((1, width), F32)
    shares = []
    for k in reversed(range(BLOCKS)):
        here = s[k * Q : (k + 1) * Q]
        later = later + here[Q - 1 : Q]
        shares = [jnp.exp2(later - here)] + shares
    xw = (rows_of(x_ref).astype(F32) * jnp.concatenate(shares, axis=0)).astype(BF16)
    state[...] = state[...] * jnp.exp2(later) + dot(folded(b_ref), xw, ((0,), (0,)))
    total[...] += later

    @pl.when(step == pl.num_programs(0) - 1)
    def _():
        end_ref[:N] = state[...].astype(BF16)
        end_ref[N:] = in_pieces(total[...])


def end_states(part, first, msg, sums=None):
    slabs, _, width = first.shape
    shape = (N + PIECES, width)
    at = (ROWS + HALF) // HEADS
    d_spec = pl.BlockSpec((SLABS, HEADS, ROWS), lambda i: (i, at, 0))
    out_specs = [pl.BlockSpec(shape, lambda i: (0, 0))]
    out_shape = [jax.ShapeDtypeStruct(shape, BF16)]
    if part == 0:
        out_specs.append(flat_spec(LANES))
        out_shape.append(jax.ShapeDtypeStruct((slabs * ROWS, LANES), BF16))
    return call(
        functools.partial(states_kernel, part),
        "states%d" % part,
        (2**30, 5, 2**20),
        grid=(slabs // SLABS,),
        in_specs=[x_spec(width), bc_spec(width), d_spec if part == 0 else flat_spec(LANES)],
        out_specs=out_specs,
        out_shape=out_shape,
        scratch_shapes=[pltpu.VMEM((N, width), F32), pltpu.VMEM((1, width), F32)],
    )(msg, first, first if part == 0 else sums)


def gain_row(part, gain_ref, width):
    head = lax.broadcasted_iota(jnp.int32, (1, width), 1) // P_SIZE
    row = jnp.zeros((1, width), F32)
    for h in range(HEADS // PARTS):
        row = jnp.where(head == h, gain_ref[part * (HEADS // PARTS) + h], row)
    return row


def own_tokens(part, x_ref, b_ref, c_ref, sums_ref, gain_ref, state, write):
    width = x_ref.shape[2]
    t = lax.broadcasted_iota(jnp.int32, (Q, Q), 0)
    u = lax.broadcasted_iota(jnp.int32, (Q, Q), 1)
    gain = gain_row(part, gain_ref, width)
    x_all = rows_of(x_ref).astype(F32)
    b_all = folded(b_ref)
    c_all = folded(c_ref)
    s_all = spread_sums(part, sums_ref[...], width)
    for k in range(BLOCKS):
        block = slice(k * Q, (k + 1) * Q)
        xf, b, c, s = x_all[block], b_all[block], c_all[block], s_all[block]
        end = s[Q - 1 : Q]
        scores = jnp.where(t >= u, dot(c, b, ((1,), (1,))), 0.0).astype(BF16)
        before = state[...]
        rest = dot(c, before.astype(BF16), ((1,), (0,))) * jnp.exp2(s) + gain * xf
        state[...] = before * jnp.exp2(end) + dot(
            b, (xf * jnp.exp2(end - s)).astype(BF16), ((0,), (0,))
        )
        for i in range(Q // SUB):
            here = slice(i * SUB, (i + 1) * SUB)
            upto = (i + 1) * SUB
            mid = s[i * SUB + SUB // 2 - 1 : i * SUB + SUB // 2]
            xw = (xf[:upto] * jnp.exp2(mid - s[:upto])).astype(BF16)
            inner = dot(scores[here, :upto], xw, ((1,), (0,))) * jnp.exp2(s[here] - mid)
            write(k * Q + i * SUB, inner + rest[here])


def weigh_ends(me, tail_ref, weights):
    later = jnp.zeros((1, weights.shape[1]), F32)
    for k in reversed(range(tail_ref.shape[0])):
        before = k < me
        weights[k : k + 1] = jnp.where(before, jnp.exp2(later), 0.0)
        later = later + jnp.where(before, of_pieces(tail_ref[k]), 0.0)


def load_start(loads, me_ref, ends_ref, tail_ref, weights, state):
    step = pl.program_id(0)
    rows = ends_ref.shape[1]

    @pl.when(step == 0)
    def _():
        weigh_ends(me_ref[0], tail_ref, weights)

    @pl.when(step < loads)
    def _():
        half = rows // 2
        for j in range(2):
            some = slice(j * half, (j + 1) * half)
            whole = jnp.zeros((half, ends_ref.shape[2]), F32)
            for k in range(ends_ref.shape[0]):
                whole = whole + ends_ref[k, some].astype(F32) * weights[k : k + 1]
            at = pl.multiple_of(step * rows + j * half, half)
            state[pl.ds(at, half), :] = whole.astype(state.dtype)


LOADS = 4


def ends_specs(ends):
    shards, _, width = ends.shape
    rows = N // LOADS
    return [
        pl.BlockSpec((shards, rows, width), lambda i: (0, jnp.minimum(i, LOADS - 1), 0)),
        pl.BlockSpec((shards, PIECES, width), lambda i: (0, N // PIECES, 0)),
    ]


def mix_kernel(part, me_ref, gain_ref, ends_ref, tail_ref, x_ref, b_ref, c_ref, sums_ref, out_ref, state, weights):
    load_start(LOADS, me_ref, ends_ref, tail_ref, weights, state)

    def write(at, rows):
        out_ref[at // ROWS, at % ROWS : at % ROWS + rows.shape[0]] = rows.astype(BF16)

    @pl.when(pl.program_id(0) >= LOADS)
    def _():
        own_tokens(part, x_ref, b_ref, c_ref, sums_ref, gain_ref, state, write)


def mix(part, me, ends, first, second, sums, gains):
    slabs, _, width = first.shape
    return call(
        functools.partial(mix_kernel, part),
        "mix%d" % part,
        (4 * 2**30, 14, 2**22),
        grid=(LOADS + slabs // SLABS,),
        in_specs=[smem_spec()] * 2
        + ends_specs(ends)
        + [
            x_spec(width, LOADS),
            bc_spec(width, LOADS),
            bc_spec(width, LOADS),
            flat_spec(LANES, LOADS),
        ],
        out_specs=x_spec(width, LOADS),
        out_shape=jax.ShapeDtypeStruct((slabs, ROWS, width), BF16),
        scratch_shapes=[pltpu.VMEM((N, width), F32), pltpu.VMEM((ends.shape[0], width), F32)],
    )(me, gains, ends, ends, (first, second)[part], first, second, sums)


def inside_kernel(part, gain_ref, x_ref, b_ref, c_ref, sums_ref, out_ref, state):
    @pl.when(pl.program_id(0) == 0)
    def _():
        state[...] = jnp.zeros_like(state)

    def write(at, rows):
        out_ref[at : at + rows.shape[0]] = rows.astype(out_ref.dtype)

    own_tokens(part, x_ref, b_ref, c_ref, sums_ref, gain_ref, state, write)


def inside(part, first, second, sums, gains):
    slabs, _, width = first.shape
    return call(
        functools.partial(inside_kernel, part),
        "inside%d" % part,
        (4 * 2**30, 14, 2**22),
        grid=(slabs // SLABS,),
        in_specs=[
            smem_spec(),
            x_spec(width),
            bc_spec(width),
            bc_spec(width),
            flat_spec(LANES),
        ],
        out_specs=flat_spec(width),
        out_shape=jax.ShapeDtypeStruct((slabs * ROWS, width), F32),
        scratch_shapes=[pltpu.VMEM((N, width), F32)],
    )(gains, (first, second)[part], first, second, sums)


def join_kernel(part, me_ref, ends_ref, tail_ref, c_ref, sums_ref, own_ref, out_ref, start, weights, total):
    step = pl.program_id(0)
    width = own_ref.shape[1]
    load_start(LOADS, me_ref, ends_ref, tail_ref, weights, start)

    @pl.when(step == 0)
    def _():
        total[...] = jnp.zeros_like(total)

    @pl.when(step >= LOADS)
    def _():
        s = spread_sums(part, sums_ref[...], width)
        outer = dot(folded(c_ref), start[...], ((1,), (0,)))
        since = total[...]
        for k in range(BLOCKS):
            here = s[k * Q : (k + 1) * Q]
            for j in range(Q // ROWS):
                some = slice(j * ROWS, (j + 1) * ROWS)
                at = slice(k * Q + j * ROWS, k * Q + (j + 1) * ROWS)
                out_ref[at.start // ROWS] = (
                    own_ref[at] + outer[at] * jnp.exp2(here[some] + since)
                ).astype(BF16)
            since = since + here[Q - 1 : Q]
        total[...] = since


def join(part, me, ends, first, second, sums, own):
    slabs, _, width = first.shape
    return call(
        functools.partial(join_kernel, part),
        "join%d" % part,
        (2**30, 12, 2**20),
        grid=(LOADS + slabs // SLABS,),
        in_specs=[smem_spec()]
        + ends_specs(ends)
        + [bc_spec(width, LOADS), flat_spec(LANES, LOADS), flat_spec(width, LOADS)],
        out_specs=x_spec(width, LOADS),
        out_shape=jax.ShapeDtypeStruct((slabs, ROWS, width), BF16),
        scratch_shapes=[
            pltpu.VMEM((N, width), BF16),
            pltpu.VMEM((ends.shape[0], width), F32),
            pltpu.VMEM((1, width), F32),
        ],
    )(me, ends, ends, second, sums, own)


def unpack_kernel(part, *refs):
    y_ref, out_ref, sems = refs[0], refs[-2], refs[-1]
    width = y_ref.shape[2]
    copies = []
    for k in range(y_ref.shape[0]):
        at = (PARTS * k + part) * width
        copies.append(
            pltpu.make_async_copy(y_ref.at[k], out_ref.at[:, at : at + width], sems.at[k])
        )
    for copy in copies:
        copy.start()
    for copy in copies:
        copy.wait()


def unpack(part, y, before=()):
    n_head, rows, width = y.shape
    return call(
        functools.partial(unpack_kernel, part),
        "unpack%d" % part,
        (0, 4, 0),
        in_specs=[pl.BlockSpec(memory_space=pltpu.VMEM)]
        + [pl.BlockSpec(memory_space=pl.ANY)] * len(before),
        out_specs=pl.BlockSpec(memory_space=pl.ANY),
        out_shape=jax.ShapeDtypeStruct((rows, n_head * PARTS * width), BF16),
        scratch_shapes=[pltpu.SemaphoreType.DMA((n_head,))],
        input_output_aliases={1: 0} if before else {},
    )(y, *before)


def exchange(msg):
    return lax.all_to_all(msg, "head", split_axis=0, concat_axis=0, tiled=True)


def local(tokens, b_proj, c_proj, log_decay, bypass_gain_vector):
    n_head = lax.axis_size("head")
    me = lax.axis_index("ctx").astype(jnp.int32).reshape(1)
    gains = bypass_gain_vector
    after = lax.optimization_barrier
    packed0, packed1 = pack(tokens, b_proj, c_proj, log_decay, n_head)
    first = exchange(packed0)
    packed1, first = after((packed1, first))
    second = exchange(packed1)
    end0, sums = end_states(0, first, first)
    ends0 = lax.all_gather(end0, "ctx")

    (end1,) = end_states(1, first, second, sums)
    ends1 = lax.all_gather(end1, "ctx")
    second, end1 = after((second, end1))
    mixed0 = mix(0, me, ends0, first, second, sums, gains)
    second, mixed0 = after((second, mixed0))
    y0 = exchange(mixed0)

    own1 = inside(1, first, second, sums, gains)
    mixed1 = join(1, me, ends1, first, second, sums, own1)
    mixed1, y0 = after((mixed1, y0))
    out = unpack(0, y0)
    return unpack(1, exchange(mixed1), (out,))


def solution(mesh):
    rows = P(("ctx", "head"), None)
    return jax.shard_map(
        local,
        mesh=mesh,
        in_specs=(rows, rows, rows, rows, P("head")),
        out_specs=rows,
        check_vma=False,
    )
```

```python
import functools

import jax
import jax.numpy as jnp
from jax import lax
from jax.experimental import pallas as pl
from jax.experimental.pallas import tpu as pltpu
from jax.sharding import PartitionSpec as P

P_SIZE = 64
N = 256
Q = 256
SUB = 64
PART_HEADS = (10, 6)
ROWS = 128
HALF = ROWS // 2
HEADS = 16
SLABS = 4
LANES = 128
PIECES = 16
CORES = 2
LOG2E = 1.4426950408889634
F32 = jnp.float32
BF16 = jnp.bfloat16
VMEM_LIMIT = 60 * 1024 * 1024


def dot(a, b, dims):
    return lax.dot_general(a, b, (dims, ((), ())), preferred_element_type=F32)


def call(kernel, name, cost, limit=VMEM_LIMIT, **kwargs):
    flops, mib, exps = cost
    return pl.pallas_call(
        kernel,
        name=name,
        compiler_params=pltpu.CompilerParams(vmem_limit_bytes=limit),
        cost_estimate=pl.CostEstimate(
            flops=flops, bytes_accessed=mib * 2**20, transcendentals=exps
        ),
        **kwargs,
    )


def first_head(part):
    return sum(PART_HEADS[:part])


def pack_kernel(x_ref, b_ref, c_ref, d_ref, first_ref, second_ref):
    dests, _, wide = first_ref.shape
    narrow = second_ref.shape[2]
    turned = jnp.transpose(d_ref[...].astype(F32)).astype(BF16)
    turned = jnp.where(pl.program_id(0) % 2 == 0, turned[: 4 * HEADS], turned[4 * HEADS :])
    low, high = slice(0, LANES), slice(LANES, 2 * LANES)
    for k in range(dests):
        cols = slice((k // 2) * N, (k // 2 + 1) * N)
        at = k * (wide + narrow)
        first_ref[k, :ROWS] = x_ref[:, at : at + wide]
        first_ref[k, ROWS:, :N] = b_ref[:HALF, cols]
        first_ref[k, ROWS:, N : 2 * N] = b_ref[HALF:, cols]
        first_ref[k, ROWS : ROWS + HEADS, 2 * N :] = turned[k * HEADS : (k + 1) * HEADS]
        first_ref[k, ROWS + HEADS :, 2 * N :] = jnp.zeros((HALF - HEADS, LANES), BF16)
        second_ref[k, :ROWS] = x_ref[:, at + wide : at + wide + narrow]
        second_ref[k, ROWS : ROWS + HALF, :N] = c_ref[:HALF, cols]
        rest = c_ref[HALF:, cols]
        second_ref[k, ROWS : ROWS + HALF, N:] = rest[:, low]
        second_ref[k, ROWS + HALF :, low] = rest[: HALF // 2, high]
        second_ref[k, ROWS + HALF :, high] = rest[HALF // 2 :, high]
        second_ref[k, ROWS + HALF :, N:] = jnp.zeros((HALF // 2, LANES), BF16)


def pack(tokens, b_proj, c_proj, log_decay, n_head):
    cols = tokens.shape[1]
    widths = [heads * P_SIZE for heads in PART_HEADS]
    heights = (ROWS + HALF, ROWS + HALF + HALF // 2)
    shapes = list(zip(heights, widths))
    return call(
        pack_kernel,
        "pack",
        (0, 12, 0),
        grid=(n_head // 4,),
        in_specs=[
            pl.BlockSpec((ROWS, 4 * cols // n_head), lambda i: (0, i)),
            pl.BlockSpec((ROWS, 2 * N), lambda i: (0, i)),
            pl.BlockSpec((ROWS, 2 * N), lambda i: (0, i)),
            pl.BlockSpec((ROWS, ROWS), lambda i: (0, i // 2)),
        ],
        out_specs=[pl.BlockSpec((4,) + shape, lambda i: (i, 0, 0)) for shape in shapes],
        out_shape=[jax.ShapeDtypeStruct((n_head,) + shape, BF16) for shape in shapes],
    )(tokens, b_proj, c_proj, log_decay)


def b_rows(ref):
    pieces = []
    for k in range(ref.shape[0]):
        pieces += [ref[k, :, :N], ref[k, :, N:]]
    return jnp.concatenate(pieces, axis=0)


def c_rows(ref, more_ref):
    pieces = []
    for k in range(ref.shape[0]):
        rest = jnp.concatenate([more_ref[k, :, :LANES], more_ref[k, :, LANES:N]], axis=0)
        pieces += [ref[k, :, :N], jnp.concatenate([ref[k, :, N:], rest], axis=1)]
    return jnp.concatenate(pieces, axis=0)


def rows_of(ref):
    return jnp.concatenate([ref[k] for k in range(ref.shape[0])], axis=0)


def three(whole):
    high = whole.astype(BF16).astype(F32)
    mid = (whole - high).astype(BF16).astype(F32)
    return high, mid, whole - high - mid


def in_pieces(whole):
    high, mid, low = three(whole)
    row = lax.broadcasted_iota(jnp.int32, (PIECES, whole.shape[1]), 0)
    out = jnp.where(row == 0, high, jnp.where(row == 1, mid, jnp.where(row == 2, low, 0.0)))
    return out.astype(BF16)


def of_pieces(rows):
    return jnp.sum(rows.astype(F32), axis=0, keepdims=True)


def block_sums(d_ref, block):
    turned = jnp.concatenate([d_ref[2 * block], d_ref[2 * block + 1]], axis=1)
    u = lax.broadcasted_iota(jnp.int32, (Q, Q), 0)
    t = lax.broadcasted_iota(jnp.int32, (Q, Q), 1)
    upper = (u <= t).astype(F32).astype(BF16)
    sums = dot(turned, upper, ((1,), (0,))) * LOG2E
    rest = jnp.zeros((LANES - 3 * HEADS, Q), F32)
    return jnp.transpose(jnp.concatenate([*three(sums), rest], axis=0)).astype(BF16)


def spread_sums(part, pieces, width):
    row = lax.broadcasted_iota(jnp.int32, (LANES, width), 0)
    col = lax.broadcasted_iota(jnp.int32, (LANES, width), 1)
    head = col // P_SIZE + first_head(part)
    taken = jnp.logical_and(row % HEADS == head, row < 3 * HEADS)
    return dot(pieces, taken.astype(F32).astype(BF16), ((1,), (0,)))


def step_of(i, shift):
    return jnp.maximum(i - shift, 0)


def x_spec(width, shift=0):
    return pl.BlockSpec((SLABS, ROWS, width), lambda i: (step_of(i, shift), 0, 0))


def b_spec(shift=0):
    return pl.BlockSpec((SLABS, HALF, 2 * N), lambda i: (step_of(i, shift), ROWS // HALF, 0))


def c_specs(shift=0):
    width = PART_HEADS[1] * P_SIZE
    return [
        pl.BlockSpec((SLABS, HALF, width), lambda i: (step_of(i, shift), ROWS // HALF, 0)),
        pl.BlockSpec(
            (SLABS, HALF // 2, width),
            lambda i: (step_of(i, shift), 2 * (ROWS + HALF) // HALF, 0),
        ),
    ]


def flat_spec(width, shift=0):
    return pl.BlockSpec((SLABS * ROWS, width), lambda i: (step_of(i, shift), 0))


def smem_spec():
    return pl.BlockSpec(memory_space=pltpu.SMEM)


BLOCKS = SLABS * ROWS // Q


def states_kernel(part, *refs):
    if part == 0:
        core_ref, x_ref, b_ref, d_ref, keep_ref, send_ref, sums_ref, state, total = refs
    else:
        core_ref, x_ref, b_ref, sums_ref, keep_ref, send_ref, state, total = refs
    step = pl.program_id(0)
    width = x_ref.shape[2]

    @pl.when(step == 0)
    def _():
        state[...] = jnp.zeros_like(state)
        total[...] = jnp.zeros_like(total)

    if part == 0:
        pieces = jnp.concatenate([block_sums(d_ref, k) for k in range(BLOCKS)], axis=0)
        sums_ref[...] = pieces
    else:
        pieces = sums_ref[...]
    s = spread_sums(part, pieces, width)
    later = jnp.zeros((1, width), F32)
    shares = []
    for k in reversed(range(BLOCKS)):
        here = s[k * Q : (k + 1) * Q]
        later = later + here[Q - 1 : Q]
        shares = [jnp.exp2(later - here)] + shares
    xw = (rows_of(x_ref).astype(F32) * jnp.concatenate(shares, axis=0)).astype(BF16)
    state[...] = state[...] * jnp.exp2(later) + dot(b_rows(b_ref), xw, ((0,), (0,)))
    total[...] += later

    @pl.when(step == pl.num_programs(0) - 1)
    def _():
        pieces = in_pieces(total[...])
        top, low = state[: N // 2], state[N // 2 :]
        first = core_ref[0] == 0
        keep_ref[: N // 2] = jnp.where(first, top, low).astype(BF16)
        send_ref[: N // 2] = jnp.where(first, low, top).astype(BF16)
        keep_ref[N // 2 :] = pieces
        send_ref[N // 2 :] = pieces


def end_states(part, core, first, msg, sums=None):
    slabs, _, width = msg.shape
    shape = (N // 2 + PIECES, width)
    d_spec = pl.BlockSpec((SLABS, HEADS, LANES), lambda i: (i, ROWS // HEADS, 2 * N // LANES))
    out_specs = [pl.BlockSpec(shape, lambda i: (0, 0))] * 2
    out_shape = [jax.ShapeDtypeStruct(shape, BF16)] * 2
    if part == 0:
        out_specs.append(flat_spec(LANES))
        out_shape.append(jax.ShapeDtypeStruct((slabs * ROWS, LANES), BF16))
    return call(
        functools.partial(states_kernel, part),
        "states%d" % part,
        (2**30, 5, 2**20),
        grid=(slabs // SLABS,),
        in_specs=[
            smem_spec(),
            x_spec(width),
            b_spec(),
            d_spec if part == 0 else flat_spec(LANES),
        ],
        out_specs=out_specs,
        out_shape=out_shape,
        scratch_shapes=[pltpu.VMEM((N, width), F32), pltpu.VMEM((1, width), F32)],
    )(core, msg, first, first if part == 0 else sums)


def halves(core_ref, keep_ref, got_ref):
    first = core_ref[0] == 0
    keep, got = keep_ref[...].astype(F32), got_ref[...].astype(F32)
    early, late = jnp.where(first, keep, got), jnp.where(first, got, keep)
    rows = N // 2
    return early[:rows], of_pieces(early[rows:]), late[:rows], of_pieces(late[rows:])


def chip_kernel(core_ref, keep_ref, got_ref, out_ref):
    early, early_total, late, late_total = halves(core_ref, keep_ref, got_ref)
    out_ref[: N // 2] = (early * jnp.exp2(late_total) + late).astype(BF16)
    out_ref[N // 2 :] = in_pieces(early_total + late_total)


def chip_state(part, core, keep, got):
    return call(
        chip_kernel,
        "chip%d" % part,
        (2**18, 1, 0),
        limit=16 * 1024 * 1024,
        in_specs=[smem_spec()] + [pl.BlockSpec(memory_space=pltpu.VMEM)] * 2,
        out_specs=pl.BlockSpec(memory_space=pltpu.VMEM),
        out_shape=jax.ShapeDtypeStruct(keep.shape, BF16),
    )(core, keep, got)


def start_kernel(core_ref, chip_ref, keep_ref, got_ref, *refs):
    mine_ref, theirs_ref, state = refs[-3:]
    others = refs[:-3]
    state[...] = jnp.zeros_like(state)
    for k in reversed(range(len(others))):

        @pl.when(k + 1 <= chip_ref[0])
        def _():
            ref = others[k]
            state[...] = state[...] * jnp.exp2(of_pieces(ref[N // 2 :])) + ref[: N // 2].astype(F32)

    early, early_total, _, _ = halves(core_ref, keep_ref, got_ref)
    before = state[...]
    after = before * jnp.exp2(early_total) + early
    first = core_ref[0] == 0
    mine_ref[...] = jnp.where(first, before, after).astype(BF16)
    theirs_ref[...] = jnp.where(first, after, before).astype(BF16)


def start_state(part, core, chip, keep, got, others):
    shape = (N // 2, keep.shape[1])
    vmem = pl.BlockSpec(memory_space=pltpu.VMEM)
    return call(
        start_kernel,
        "start%d" % part,
        (2**20, 2, 0),
        limit=16 * 1024 * 1024,
        in_specs=[smem_spec()] * 2 + [vmem] * (2 + len(others)),
        out_specs=[vmem] * 2,
        out_shape=[jax.ShapeDtypeStruct(shape, BF16)] * 2,
        scratch_shapes=[pltpu.VMEM(shape, F32)],
    )(core, chip, keep, got, *others)


def incoming(part, core, chip, keep, send, beside=None):
    shards = lax.axis_size("ctx")
    swap = [(i, i ^ 1) for i in range(shards)]
    ahead = [(i, (i + CORES) % shards) for i in range(shards)]
    back = [(i, (i - CORES) % shards) for i in range(shards)]
    got = lax.ppermute(send, "ctx", swap)
    own = chip_state(part, core, keep, got)
    chips = shards // CORES
    forward, backward = [own], [own]
    for step in range(chips // 2):
        forward.append(lax.ppermute(forward[-1], "ctx", ahead))
        if step < chips - 1 - chips // 2:
            backward.append(lax.ppermute(backward[-1], "ctx", back))
        if step == 0 and beside is not None:
            forward[-1], backward[-1], beside = lax.optimization_barrier(
                (forward[-1], backward[-1], beside)
            )
    mine, theirs = start_state(part, core, chip, keep, got, forward[1:] + backward[:0:-1])
    return mine, lax.ppermute(theirs, "ctx", swap), beside


def gain_row(part, gain_ref, width):
    head = lax.broadcasted_iota(jnp.int32, (1, width), 1) // P_SIZE
    row = jnp.zeros((1, width), F32)
    for h in range(PART_HEADS[part]):
        row = jnp.where(head == h, gain_ref[first_head(part) + h], row)
    return row


def own_tokens(part, x_ref, b_ref, c_refs, sums_ref, gain_ref, state, write):
    width = x_ref.shape[2]
    t = lax.broadcasted_iota(jnp.int32, (Q, Q), 0)
    u = lax.broadcasted_iota(jnp.int32, (Q, Q), 1)
    gain = gain_row(part, gain_ref, width)
    x_all = rows_of(x_ref).astype(F32)
    b_all = b_rows(b_ref)
    c_all = c_rows(*c_refs)
    s_all = spread_sums(part, sums_ref[...], width)
    for k in range(BLOCKS):
        block = slice(k * Q, (k + 1) * Q)
        xf, b, c, s = x_all[block], b_all[block], c_all[block], s_all[block]
        end = s[Q - 1 : Q]
        scores = jnp.where(t >= u, dot(c, b, ((1,), (1,))), 0.0).astype(BF16)
        before = state[...]
        rest = dot(c, before.astype(BF16), ((1,), (0,))) * jnp.exp2(s) + gain * xf
        state[...] = before * jnp.exp2(end) + dot(
            b, (xf * jnp.exp2(end - s)).astype(BF16), ((0,), (0,))
        )
        for i in range(Q // SUB):
            here = slice(i * SUB, (i + 1) * SUB)
            upto = (i + 1) * SUB
            mid = s[i * SUB + SUB // 2 - 1 : i * SUB + SUB // 2]
            xw = (xf[:upto] * jnp.exp2(mid - s[:upto])).astype(BF16)
            inner = dot(scores[here, :upto], xw, ((1,), (0,))) * jnp.exp2(s[here] - mid)
            write(k * Q + i * SUB, inner + rest[here])


def start_from(core_ref, mine_ref, got_ref, state):
    @pl.when(pl.program_id(0) == 0)
    def _():
        first = core_ref[0] == 0
        mine, got = mine_ref[...].astype(F32), got_ref[...].astype(F32)
        state[: N // 2] = jnp.where(first, mine, got).astype(state.dtype)
        state[N // 2 :] = jnp.where(first, got, mine).astype(state.dtype)


def half_spec(width):
    return pl.BlockSpec((N // 2, width), lambda i: (0, 0))


def mix_kernel(
    part, core_ref, gain_ref, mine_ref, got_ref, x_ref, b_ref, c_ref, more_ref, sums_ref, out_ref, state
):
    start_from(core_ref, mine_ref, got_ref, state)

    def write(at, rows):
        out_ref[at // ROWS, at % ROWS : at % ROWS + rows.shape[0]] = rows.astype(BF16)

    own_tokens(part, x_ref, b_ref, (c_ref, more_ref), sums_ref, gain_ref, state, write)


def mix(part, core, mine, got, first, second, sums, gains):
    slabs, _, width = (first, second)[part].shape
    return call(
        functools.partial(mix_kernel, part),
        "mix%d" % part,
        (4 * 2**30, 14, 2**22),
        grid=(slabs // SLABS,),
        in_specs=[smem_spec()] * 2
        + [half_spec(width)] * 2
        + [x_spec(width), b_spec(), *c_specs(), flat_spec(LANES)],
        out_specs=x_spec(width),
        out_shape=jax.ShapeDtypeStruct((slabs, ROWS, width), BF16),
        scratch_shapes=[pltpu.VMEM((N, width), F32)],
    )(core, gains, mine, got, (first, second)[part], first, second, second, sums)


def inside_kernel(part, gain_ref, x_ref, b_ref, c_ref, more_ref, sums_ref, out_ref, state):
    @pl.when(pl.program_id(0) == 0)
    def _():
        state[...] = jnp.zeros_like(state)

    def write(at, rows):
        out_ref[at : at + rows.shape[0]] = rows.astype(out_ref.dtype)

    own_tokens(part, x_ref, b_ref, (c_ref, more_ref), sums_ref, gain_ref, state, write)


def inside(part, first, second, sums, gains):
    slabs, _, width = (first, second)[part].shape
    return call(
        functools.partial(inside_kernel, part),
        "inside%d" % part,
        (4 * 2**30, 14, 2**22),
        grid=(slabs // SLABS,),
        in_specs=[
            smem_spec(),
            x_spec(width),
            b_spec(),
            *c_specs(),
            flat_spec(LANES),
        ],
        out_specs=flat_spec(width),
        out_shape=jax.ShapeDtypeStruct((slabs * ROWS, width), BF16),
        scratch_shapes=[pltpu.VMEM((N, width), F32)],
    )(gains, (first, second)[part], first, second, second, sums)


def join_kernel(
    part, core_ref, mine_ref, got_ref, c_ref, more_ref, sums_ref, own_ref, out_ref, start, total
):
    width = own_ref.shape[1]
    start_from(core_ref, mine_ref, got_ref, start)

    @pl.when(pl.program_id(0) == 0)
    def _():
        total[...] = jnp.zeros_like(total)

    s = spread_sums(part, sums_ref[...], width)
    outer = dot(c_rows(c_ref, more_ref), start[...], ((1,), (0,)))
    since = total[...]
    for k in range(BLOCKS):
        here = s[k * Q : (k + 1) * Q]
        for j in range(Q // ROWS):
            some = slice(j * ROWS, (j + 1) * ROWS)
            at = slice(k * Q + j * ROWS, k * Q + (j + 1) * ROWS)
            out_ref[at.start // ROWS] = (
                own_ref[at].astype(F32) + outer[at] * jnp.exp2(here[some] + since)
            ).astype(BF16)
        since = since + here[Q - 1 : Q]
    total[...] = since


def join(part, core, mine, got, first, second, sums, own):
    slabs, _, width = (first, second)[part].shape
    return call(
        functools.partial(join_kernel, part),
        "join%d" % part,
        (2**30, 8, 2**20),
        grid=(slabs // SLABS,),
        in_specs=[smem_spec()]
        + [half_spec(width)] * 2
        + [*c_specs(), flat_spec(LANES), flat_spec(width)],
        out_specs=x_spec(width),
        out_shape=jax.ShapeDtypeStruct((slabs, ROWS, width), BF16),
        scratch_shapes=[pltpu.VMEM((N, width), BF16), pltpu.VMEM((1, width), F32)],
    )(core, mine, got, second, second, sums, own)


def unpack_kernel(part, *refs):
    y_ref, out_ref, sems = refs[0], refs[-2], refs[-1]
    width = y_ref.shape[2]
    copies = []
    for k in range(y_ref.shape[0]):
        at = (k * HEADS + first_head(part)) * P_SIZE
        copies.append(
            pltpu.make_async_copy(y_ref.at[k], out_ref.at[:, at : at + width], sems.at[k])
        )
    for copy in copies:
        copy.start()
    for copy in copies:
        copy.wait()


def unpack(part, y, before=()):
    n_head, rows, width = y.shape
    return call(
        functools.partial(unpack_kernel, part),
        "unpack%d" % part,
        (0, 4, 0),
        limit=16 * 1024 * 1024,
        in_specs=[pl.BlockSpec(memory_space=pltpu.VMEM)]
        + [pl.BlockSpec(memory_space=pl.ANY)] * len(before),
        out_specs=pl.BlockSpec(memory_space=pl.ANY),
        out_shape=jax.ShapeDtypeStruct((rows, n_head * HEADS * P_SIZE), BF16),
        scratch_shapes=[pltpu.SemaphoreType.DMA((n_head,))],
        input_output_aliases={1: 0} if before else {},
    )(y, *before)


def exchange(msg):
    return lax.all_to_all(msg, "head", split_axis=0, concat_axis=0, tiled=True)


def local(tokens, b_proj, c_proj, log_decay, bypass_gain_vector):
    n_head = lax.axis_size("head")
    me = lax.axis_index("ctx").astype(jnp.int32).reshape(1)
    core, chip = me % CORES, me // CORES
    gains = bypass_gain_vector
    after = lax.optimization_barrier
    packed0, packed1 = pack(tokens, b_proj, c_proj, log_decay, n_head)
    first = exchange(packed0)
    packed1, first = after((packed1, first))
    second = exchange(packed1)
    keep0, send0, sums = end_states(0, core, first, first)
    mine0, got0, _ = incoming(0, core, chip, keep0, send0)
    mixed0 = mix(0, core, mine0, got0, first, second, sums, gains)
    second, mixed0 = after((second, mixed0))
    y0 = exchange(mixed0)

    keep1, send1 = end_states(1, core, first, second, sums)
    own1 = inside(1, first, second, sums, gains)
    mine1, got1, own1 = incoming(1, core, chip, keep1, send1, own1)
    mixed1 = join(1, core, mine1, got1, first, second, sums, own1)
    mixed1, y0 = after((mixed1, y0))
    out = unpack(0, y0)
    return unpack(1, exchange(mixed1), (out,))


def solution(mesh):
    rows = P(("ctx", "head"), None)
    return jax.shard_map(
        local,
        mesh=mesh,
        in_specs=(rows, rows, rows, rows, P("head")),
        out_specs=rows,
        check_vma=False,
    )
```

```python
import functools

import jax
import jax.numpy as jnp
from jax import lax
from jax.experimental import pallas as pl
from jax.experimental.pallas import tpu as pltpu
from jax.sharding import PartitionSpec as P

P_SIZE = 64
N = 256
Q = 256
SUB = 64
PART_HEADS = (10, 6)
ROWS = 128
HALF = ROWS // 2
HEADS = 16
SLABS = 4
LANES = 128
PIECES = 16
CORES = 2
LOG2E = 1.4426950408889634
F32 = jnp.float32
BF16 = jnp.bfloat16
VMEM_LIMIT = 60 * 1024 * 1024


def dot(a, b, dims):
    return lax.dot_general(a, b, (dims, ((), ())), preferred_element_type=F32)


def call(kernel, name, cost, limit=VMEM_LIMIT, **kwargs):
    flops, mib, exps = cost
    return pl.pallas_call(
        kernel,
        name=name,
        compiler_params=pltpu.CompilerParams(vmem_limit_bytes=limit),
        cost_estimate=pl.CostEstimate(
            flops=flops, bytes_accessed=mib * 2**20, transcendentals=exps
        ),
        **kwargs,
    )


def first_head(part):
    return sum(PART_HEADS[:part])


def pack_kernel(x_ref, b_ref, c_ref, d_ref, first_ref, second_ref):
    dests, _, wide = first_ref.shape
    narrow = second_ref.shape[2]
    turned = jnp.transpose(d_ref[...].astype(F32)).astype(BF16)
    turned = jnp.where(pl.program_id(0) % 2 == 0, turned[: 4 * HEADS], turned[4 * HEADS :])
    low, high = slice(0, LANES), slice(LANES, 2 * LANES)
    for k in range(dests):
        cols = slice((k // 2) * N, (k // 2 + 1) * N)
        at = k * (wide + narrow)
        first_ref[k, :ROWS] = x_ref[:, at : at + wide]
        first_ref[k, ROWS:, :N] = b_ref[:HALF, cols]
        first_ref[k, ROWS:, N : 2 * N] = b_ref[HALF:, cols]
        first_ref[k, ROWS : ROWS + HEADS, 2 * N :] = turned[k * HEADS : (k + 1) * HEADS]
        first_ref[k, ROWS + HEADS :, 2 * N :] = jnp.zeros((HALF - HEADS, LANES), BF16)
        second_ref[k, :ROWS] = x_ref[:, at + wide : at + wide + narrow]
        second_ref[k, ROWS : ROWS + HALF, :N] = c_ref[:HALF, cols]
        rest = c_ref[HALF:, cols]
        second_ref[k, ROWS : ROWS + HALF, N:] = rest[:, low]
        second_ref[k, ROWS + HALF :, low] = rest[: HALF // 2, high]
        second_ref[k, ROWS + HALF :, high] = rest[HALF // 2 :, high]
        second_ref[k, ROWS + HALF :, N:] = jnp.zeros((HALF // 2, LANES), BF16)


def pack(tokens, b_proj, c_proj, log_decay, n_head):
    cols = tokens.shape[1]
    widths = [heads * P_SIZE for heads in PART_HEADS]
    heights = (ROWS + HALF, ROWS + HALF + HALF // 2)
    shapes = list(zip(heights, widths))
    return call(
        pack_kernel,
        "pack",
        (0, 12, 0),
        grid=(n_head // 4,),
        in_specs=[
            pl.BlockSpec((ROWS, 4 * cols // n_head), lambda i: (0, i)),
            pl.BlockSpec((ROWS, 2 * N), lambda i: (0, i)),
            pl.BlockSpec((ROWS, 2 * N), lambda i: (0, i)),
            pl.BlockSpec((ROWS, ROWS), lambda i: (0, i // 2)),
        ],
        out_specs=[pl.BlockSpec((4,) + shape, lambda i: (i, 0, 0)) for shape in shapes],
        out_shape=[jax.ShapeDtypeStruct((n_head,) + shape, BF16) for shape in shapes],
    )(tokens, b_proj, c_proj, log_decay)


def b_rows(ref):
    pieces = []
    for k in range(ref.shape[0]):
        pieces += [ref[k, :, :N], ref[k, :, N:]]
    return jnp.concatenate(pieces, axis=0)


def c_rows(ref, more_ref):
    pieces = []
    for k in range(ref.shape[0]):
        rest = jnp.concatenate([more_ref[k, :, :LANES], more_ref[k, :, LANES:N]], axis=0)
        pieces += [ref[k, :, :N], jnp.concatenate([ref[k, :, N:], rest], axis=1)]
    return jnp.concatenate(pieces, axis=0)


def rows_of(ref):
    return jnp.concatenate([ref[k] for k in range(ref.shape[0])], axis=0)


def three(whole):
    high = whole.astype(BF16).astype(F32)
    mid = (whole - high).astype(BF16).astype(F32)
    return high, mid, whole - high - mid


def in_pieces(whole):
    high, mid, low = three(whole)
    row = lax.broadcasted_iota(jnp.int32, (PIECES, whole.shape[1]), 0)
    out = jnp.where(row == 0, high, jnp.where(row == 1, mid, jnp.where(row == 2, low, 0.0)))
    return out.astype(BF16)


def of_pieces(rows):
    return jnp.sum(rows.astype(F32), axis=0, keepdims=True)


def block_sums(d_ref, block):
    turned = jnp.concatenate([d_ref[2 * block], d_ref[2 * block + 1]], axis=1)
    u = lax.broadcasted_iota(jnp.int32, (Q, Q), 0)
    t = lax.broadcasted_iota(jnp.int32, (Q, Q), 1)
    upper = (u <= t).astype(F32).astype(BF16)
    sums = dot(turned, upper, ((1,), (0,))) * LOG2E
    rest = jnp.zeros((LANES - 3 * HEADS, Q), F32)
    return jnp.transpose(jnp.concatenate([*three(sums), rest], axis=0)).astype(BF16)


def spread_sums(part, pieces, width):
    row = lax.broadcasted_iota(jnp.int32, (LANES, width), 0)
    col = lax.broadcasted_iota(jnp.int32, (LANES, width), 1)
    head = col // P_SIZE + first_head(part)
    taken = jnp.logical_and(row % HEADS == head, row < 3 * HEADS)
    return dot(pieces, taken.astype(F32).astype(BF16), ((1,), (0,)))


def step_of(i, shift):
    return jnp.maximum(i - shift, 0)


def x_spec(width, shift=0):
    return pl.BlockSpec((SLABS, ROWS, width), lambda i: (step_of(i, shift), 0, 0))


def b_spec(shift=0):
    return pl.BlockSpec((SLABS, HALF, 2 * N), lambda i: (step_of(i, shift), ROWS // HALF, 0))


def c_specs(shift=0):
    width = PART_HEADS[1] * P_SIZE
    return [
        pl.BlockSpec((SLABS, HALF, width), lambda i: (step_of(i, shift), ROWS // HALF, 0)),
        pl.BlockSpec(
            (SLABS, HALF // 2, width),
            lambda i: (step_of(i, shift), 2 * (ROWS + HALF) // HALF, 0),
        ),
    ]


def flat_spec(width, shift=0):
    return pl.BlockSpec((SLABS * ROWS, width), lambda i: (step_of(i, shift), 0))


def smem_spec():
    return pl.BlockSpec(memory_space=pltpu.SMEM)


BLOCKS = SLABS * ROWS // Q


def states_kernel(part, *refs):
    if part == 0:
        core_ref, x_ref, b_ref, d_ref, keep_ref, send_ref, sums_ref, state, total = refs
    else:
        core_ref, x_ref, b_ref, sums_ref, keep_ref, send_ref, state, total = refs
    step = pl.program_id(0)
    width = x_ref.shape[2]

    @pl.when(step == 0)
    def _():
        state[...] = jnp.zeros_like(state)
        total[...] = jnp.zeros_like(total)

    if part == 0:
        pieces = jnp.concatenate([block_sums(d_ref, k) for k in range(BLOCKS)], axis=0)
        sums_ref[...] = pieces
    else:
        pieces = sums_ref[...]
    s = spread_sums(part, pieces, width)
    later = jnp.zeros((1, width), F32)
    shares = []
    for k in reversed(range(BLOCKS)):
        here = s[k * Q : (k + 1) * Q]
        later = later + here[Q - 1 : Q]
        shares = [jnp.exp2(later - here)] + shares
    xw = (rows_of(x_ref).astype(F32) * jnp.concatenate(shares, axis=0)).astype(BF16)
    state[...] = state[...] * jnp.exp2(later) + dot(b_rows(b_ref), xw, ((0,), (0,)))
    total[...] += later

    @pl.when(step == pl.num_programs(0) - 1)
    def _():
        pieces = in_pieces(total[...])
        top, low = state[: N // 2], state[N // 2 :]
        first = core_ref[0] == 0
        keep_ref[: N // 2] = jnp.where(first, top, low).astype(BF16)
        send_ref[: N // 2] = jnp.where(first, low, top).astype(BF16)
        keep_ref[N // 2 :] = pieces
        send_ref[N // 2 :] = pieces


def end_states(part, core, first, msg, sums=None):
    slabs, _, width = msg.shape
    shape = (N // 2 + PIECES, width)
    d_spec = pl.BlockSpec((SLABS, HEADS, LANES), lambda i: (i, ROWS // HEADS, 2 * N // LANES))
    out_specs = [pl.BlockSpec(shape, lambda i: (0, 0))] * 2
    out_shape = [jax.ShapeDtypeStruct(shape, BF16)] * 2
    if part == 0:
        out_specs.append(flat_spec(LANES))
        out_shape.append(jax.ShapeDtypeStruct((slabs * ROWS, LANES), BF16))
    return call(
        functools.partial(states_kernel, part),
        "states%d" % part,
        (2**30, 5, 2**20),
        grid=(slabs // SLABS,),
        in_specs=[
            smem_spec(),
            x_spec(width),
            b_spec(),
            d_spec if part == 0 else flat_spec(LANES),
        ],
        out_specs=out_specs,
        out_shape=out_shape,
        scratch_shapes=[pltpu.VMEM((N, width), F32), pltpu.VMEM((1, width), F32)],
    )(core, msg, first, first if part == 0 else sums)


def halves(core_ref, keep_ref, got_ref):
    first = core_ref[0] == 0
    keep, got = keep_ref[...].astype(F32), got_ref[...].astype(F32)
    early, late = jnp.where(first, keep, got), jnp.where(first, got, keep)
    rows = N // 2
    return early[:rows], of_pieces(early[rows:]), late[:rows], of_pieces(late[rows:])


def chip_kernel(core_ref, keep_ref, got_ref, out_ref):
    early, early_total, late, late_total = halves(core_ref, keep_ref, got_ref)
    out_ref[: N // 2] = (early * jnp.exp2(late_total) + late).astype(BF16)
    out_ref[N // 2 :] = in_pieces(early_total + late_total)


def chip_state(part, core, keep, got):
    return call(
        chip_kernel,
        "chip%d" % part,
        (2**18, 1, 0),
        limit=16 * 1024 * 1024,
        in_specs=[smem_spec()] + [pl.BlockSpec(memory_space=pltpu.VMEM)] * 2,
        out_specs=pl.BlockSpec(memory_space=pltpu.VMEM),
        out_shape=jax.ShapeDtypeStruct(keep.shape, BF16),
    )(core, keep, got)


def start_kernel(core_ref, chip_ref, keep_ref, got_ref, *refs):
    mine_ref, theirs_ref, state = refs[-3:]
    others = refs[:-3]
    state[...] = jnp.zeros_like(state)
    for k in reversed(range(len(others))):

        @pl.when(k + 1 <= chip_ref[0])
        def _():
            ref = others[k]
            state[...] = state[...] * jnp.exp2(of_pieces(ref[N // 2 :])) + ref[: N // 2].astype(F32)

    early, early_total, _, _ = halves(core_ref, keep_ref, got_ref)
    before = state[...]
    after = before * jnp.exp2(early_total) + early
    first = core_ref[0] == 0
    mine_ref[...] = jnp.where(first, before, after).astype(BF16)
    theirs_ref[...] = jnp.where(first, after, before).astype(BF16)


def start_state(part, core, chip, keep, got, others):
    shape = (N // 2, keep.shape[1])
    vmem = pl.BlockSpec(memory_space=pltpu.VMEM)
    return call(
        start_kernel,
        "start%d" % part,
        (2**20, 2, 0),
        limit=16 * 1024 * 1024,
        in_specs=[smem_spec()] * 2 + [vmem] * (2 + len(others)),
        out_specs=[vmem] * 2,
        out_shape=[jax.ShapeDtypeStruct(shape, BF16)] * 2,
        scratch_shapes=[pltpu.VMEM(shape, F32)],
    )(core, chip, keep, got, *others)


def incoming(part, core, chip, keep, send, beside=None):
    shards = lax.axis_size("ctx")
    swap = [(i, i ^ 1) for i in range(shards)]
    ahead = [(i, (i + CORES) % shards) for i in range(shards)]
    back = [(i, (i - CORES) % shards) for i in range(shards)]
    got = lax.ppermute(send, "ctx", swap)
    own = chip_state(part, core, keep, got)
    chips = shards // CORES
    forward, backward = [own], [own]
    for step in range(chips // 2):
        forward.append(lax.ppermute(forward[-1], "ctx", ahead))
        if step < chips - 1 - chips // 2:
            backward.append(lax.ppermute(backward[-1], "ctx", back))
        if step == 0 and beside is not None:
            forward[-1], backward[-1], beside = lax.optimization_barrier(
                (forward[-1], backward[-1], beside)
            )
    mine, theirs = start_state(part, core, chip, keep, got, forward[1:] + backward[:0:-1])
    return mine, lax.ppermute(theirs, "ctx", swap), beside


def gain_row(part, gain_ref, width):
    head = lax.broadcasted_iota(jnp.int32, (1, width), 1) // P_SIZE
    row = jnp.zeros((1, width), F32)
    for h in range(PART_HEADS[part]):
        row = jnp.where(head == h, gain_ref[first_head(part) + h], row)
    return row


def own_tokens(part, x_ref, b_ref, c_refs, sums_ref, gain_ref, state, write):
    width = x_ref.shape[2]
    t = lax.broadcasted_iota(jnp.int32, (Q, Q), 0)
    u = lax.broadcasted_iota(jnp.int32, (Q, Q), 1)
    gain = gain_row(part, gain_ref, width)
    x_all = rows_of(x_ref).astype(F32)
    b_all = b_rows(b_ref)
    c_all = c_rows(*c_refs)
    s_all = spread_sums(part, sums_ref[...], width)
    for k in range(BLOCKS):
        block = slice(k * Q, (k + 1) * Q)
        xf, b, c, s = x_all[block], b_all[block], c_all[block], s_all[block]
        end = s[Q - 1 : Q]
        scores = jnp.where(t >= u, dot(c, b, ((1,), (1,))), 0.0).astype(BF16)
        before = state[...]
        rest = dot(c, before.astype(BF16), ((1,), (0,))) * jnp.exp2(s) + gain * xf
        state[...] = before * jnp.exp2(end) + dot(
            b, (xf * jnp.exp2(end - s)).astype(BF16), ((0,), (0,))
        )
        for i in range(Q // SUB):
            here = slice(i * SUB, (i + 1) * SUB)
            upto = (i + 1) * SUB
            mid = s[i * SUB + SUB // 2 - 1 : i * SUB + SUB // 2]
            xw = (xf[:upto] * jnp.exp2(mid - s[:upto])).astype(BF16)
            inner = dot(scores[here, :upto], xw, ((1,), (0,))) * jnp.exp2(s[here] - mid)
            write(k * Q + i * SUB, inner + rest[here])


def start_from(core_ref, mine_ref, got_ref, state):
    @pl.when(pl.program_id(0) == 0)
    def _():
        first = core_ref[0] == 0
        mine, got = mine_ref[...].astype(F32), got_ref[...].astype(F32)
        state[: N // 2] = jnp.where(first, mine, got).astype(state.dtype)
        state[N // 2 :] = jnp.where(first, got, mine).astype(state.dtype)


def half_spec(width):
    return pl.BlockSpec((N // 2, width), lambda i: (0, 0))


def mix_kernel(
    part, core_ref, gain_ref, mine_ref, got_ref, x_ref, b_ref, c_ref, more_ref, sums_ref, out_ref, state
):
    start_from(core_ref, mine_ref, got_ref, state)

    def write(at, rows):
        out_ref[at // ROWS, at % ROWS : at % ROWS + rows.shape[0]] = rows.astype(BF16)

    own_tokens(part, x_ref, b_ref, (c_ref, more_ref), sums_ref, gain_ref, state, write)


def mix(part, core, mine, got, first, second, sums, gains):
    slabs, _, width = (first, second)[part].shape
    return call(
        functools.partial(mix_kernel, part),
        "mix%d" % part,
        (4 * 2**30, 14, 2**22),
        grid=(slabs // SLABS,),
        in_specs=[smem_spec()] * 2
        + [half_spec(width)] * 2
        + [x_spec(width), b_spec(), *c_specs(), flat_spec(LANES)],
        out_specs=x_spec(width),
        out_shape=jax.ShapeDtypeStruct((slabs, ROWS, width), BF16),
        scratch_shapes=[pltpu.VMEM((N, width), F32)],
    )(core, gains, mine, got, (first, second)[part], first, second, second, sums)


def inside_kernel(part, gain_ref, x_ref, b_ref, c_ref, more_ref, sums_ref, out_ref, state):
    @pl.when(pl.program_id(0) == 0)
    def _():
        state[...] = jnp.zeros_like(state)

    def write(at, rows):
        out_ref[at : at + rows.shape[0]] = rows.astype(out_ref.dtype)

    own_tokens(part, x_ref, b_ref, (c_ref, more_ref), sums_ref, gain_ref, state, write)


def inside(part, first, second, sums, gains):
    slabs, _, width = (first, second)[part].shape
    return call(
        functools.partial(inside_kernel, part),
        "inside%d" % part,
        (4 * 2**30, 14, 2**22),
        grid=(slabs // SLABS,),
        in_specs=[
            smem_spec(),
            x_spec(width),
            b_spec(),
            *c_specs(),
            flat_spec(LANES),
        ],
        out_specs=flat_spec(width),
        out_shape=jax.ShapeDtypeStruct((slabs * ROWS, width), BF16),
        scratch_shapes=[pltpu.VMEM((N, width), F32)],
    )(gains, (first, second)[part], first, second, second, sums)


def join_kernel(
    part, core_ref, mine_ref, got_ref, c_ref, more_ref, sums_ref, own_ref, out_ref, start, total
):
    width = own_ref.shape[1]
    start_from(core_ref, mine_ref, got_ref, start)

    @pl.when(pl.program_id(0) == 0)
    def _():
        total[...] = jnp.zeros_like(total)

    s = spread_sums(part, sums_ref[...], width)
    outer = dot(c_rows(c_ref, more_ref), start[...], ((1,), (0,)))
    since = total[...]
    for k in range(BLOCKS):
        here = s[k * Q : (k + 1) * Q]
        for j in range(Q // ROWS):
            some = slice(j * ROWS, (j + 1) * ROWS)
            at = slice(k * Q + j * ROWS, k * Q + (j + 1) * ROWS)
            out_ref[at.start // ROWS] = (
                own_ref[at].astype(F32) + outer[at] * jnp.exp2(here[some] + since)
            ).astype(BF16)
        since = since + here[Q - 1 : Q]
    total[...] = since


def join(part, core, mine, got, first, second, sums, own):
    slabs, _, width = (first, second)[part].shape
    return call(
        functools.partial(join_kernel, part),
        "join%d" % part,
        (2**30, 8, 2**20),
        grid=(slabs // SLABS,),
        in_specs=[smem_spec()]
        + [half_spec(width)] * 2
        + [*c_specs(), flat_spec(LANES), flat_spec(width)],
        out_specs=x_spec(width),
        out_shape=jax.ShapeDtypeStruct((slabs, ROWS, width), BF16),
        scratch_shapes=[pltpu.VMEM((N, width), BF16), pltpu.VMEM((1, width), F32)],
    )(core, mine, got, second, second, sums, own)


def unpack_kernel(part, *refs):
    y_ref, out_ref, sems = refs[0], refs[-2], refs[-1]
    width = y_ref.shape[2]
    copies = []
    for k in range(y_ref.shape[0]):
        at = (k * HEADS + first_head(part)) * P_SIZE
        copies.append(
            pltpu.make_async_copy(y_ref.at[k], out_ref.at[:, at : at + width], sems.at[k])
        )
    for copy in copies:
        copy.start()
    for copy in copies:
        copy.wait()


def unpack(part, y, before=()):
    n_head, rows, width = y.shape
    return call(
        functools.partial(unpack_kernel, part),
        "unpack%d" % part,
        (0, 4, 0),
        limit=16 * 1024 * 1024,
        in_specs=[pl.BlockSpec(memory_space=pltpu.VMEM)]
        + [pl.BlockSpec(memory_space=pl.ANY)] * len(before),
        out_specs=pl.BlockSpec(memory_space=pl.ANY),
        out_shape=jax.ShapeDtypeStruct((rows, n_head * HEADS * P_SIZE), BF16),
        scratch_shapes=[pltpu.SemaphoreType.DMA((n_head,))],
        input_output_aliases={1: 0} if before else {},
    )(y, *before)


def exchange(msg):
    return lax.all_to_all(msg, "head", split_axis=0, concat_axis=0, tiled=True)


def local(tokens, b_proj, c_proj, log_decay, bypass_gain_vector):
    n_head = lax.axis_size("head")
    me = lax.axis_index("ctx").astype(jnp.int32).reshape(1)
    core, chip = me % CORES, me // CORES
    gains = bypass_gain_vector
    after = lax.optimization_barrier
    packed0, packed1 = pack(tokens, b_proj, c_proj, log_decay, n_head)
    first = exchange(packed0)
    packed1, first = after((packed1, first))
    second = exchange(packed1)
    keep0, send0, sums = end_states(0, core, first, first)
    mine0, got0, _ = incoming(0, core, chip, keep0, send0)
    keep1, send1 = end_states(1, core, first, second, sums)
    mine0, send1 = after((mine0, send1))
    mixed0 = mix(0, core, mine0, got0, first, second, sums, gains)
    y0 = exchange(mixed0)

    own1 = inside(1, first, second, sums, gains)
    mine1, got1, own1 = incoming(1, core, chip, keep1, send1, own1)
    mixed1 = join(1, core, mine1, got1, first, second, sums, own1)
    mixed1, y0 = after((mixed1, y0))
    out = unpack(0, y0)
    return unpack(1, exchange(mixed1), (out,))


def solution(mesh):
    rows = P(("ctx", "head"), None)
    return jax.shard_map(
        local,
        mesh=mesh,
        in_specs=(rows, rows, rows, rows, P("head")),
        out_specs=rows,
        check_vma=False,
    )
```

```python
import functools

import jax
import jax.numpy as jnp
from jax import lax
from jax.experimental import pallas as pl
from jax.experimental.pallas import tpu as pltpu
from jax.sharding import PartitionSpec as P

P_SIZE = 64
N = 256
Q = 256
SUB = 64
PART_HEADS = (10, 6)
ROWS = 128
HALF = ROWS // 2
HEADS = 16
SLABS = 4
LANES = 128
PIECES = 16
CORES = 2
LOG2E = 1.4426950408889634
F32 = jnp.float32
BF16 = jnp.bfloat16
VMEM_LIMIT = 60 * 1024 * 1024


def far(*arrays):
    return [pltpu.with_memory_space_constraint(x, pltpu.HBM) for x in arrays]


def dot(a, b, dims):
    return lax.dot_general(a, b, (dims, ((), ())), preferred_element_type=F32)


def call(kernel, name, cost, limit=VMEM_LIMIT, **kwargs):
    flops, mib, exps = cost
    return pl.pallas_call(
        kernel,
        name=name,
        compiler_params=pltpu.CompilerParams(vmem_limit_bytes=limit),
        cost_estimate=pl.CostEstimate(
            flops=flops, bytes_accessed=mib * 2**20, transcendentals=exps
        ),
        **kwargs,
    )


def first_head(part):
    return sum(PART_HEADS[:part])


def pack_kernel(x_ref, b_ref, c_ref, d_ref, first_ref, second_ref):
    dests, _, wide = first_ref.shape
    narrow = second_ref.shape[2]
    turned = jnp.transpose(d_ref[...].astype(F32)).astype(BF16)
    turned = jnp.where(pl.program_id(0) % 2 == 0, turned[: 4 * HEADS], turned[4 * HEADS :])
    low, high = slice(0, LANES), slice(LANES, 2 * LANES)
    for k in range(dests):
        cols = slice((k // 2) * N, (k // 2 + 1) * N)
        at = k * (wide + narrow)
        first_ref[k, :ROWS] = x_ref[:, at : at + wide]
        first_ref[k, ROWS:, :N] = b_ref[:HALF, cols]
        first_ref[k, ROWS:, N : 2 * N] = b_ref[HALF:, cols]
        first_ref[k, ROWS : ROWS + HEADS, 2 * N :] = turned[k * HEADS : (k + 1) * HEADS]
        first_ref[k, ROWS + HEADS :, 2 * N :] = jnp.zeros((HALF - HEADS, LANES), BF16)
        second_ref[k, :ROWS] = x_ref[:, at + wide : at + wide + narrow]
        second_ref[k, ROWS : ROWS + HALF, :N] = c_ref[:HALF, cols]
        rest = c_ref[HALF:, cols]
        second_ref[k, ROWS : ROWS + HALF, N:] = rest[:, low]
        second_ref[k, ROWS + HALF :, low] = rest[: HALF // 2, high]
        second_ref[k, ROWS + HALF :, high] = rest[HALF // 2 :, high]
        second_ref[k, ROWS + HALF :, N:] = jnp.zeros((HALF // 2, LANES), BF16)


def pack(tokens, b_proj, c_proj, log_decay, n_head):
    cols = tokens.shape[1]
    widths = [heads * P_SIZE for heads in PART_HEADS]
    heights = (ROWS + HALF, ROWS + HALF + HALF // 2)
    shapes = list(zip(heights, widths))
    return call(
        pack_kernel,
        "pack",
        (0, 12, 0),
        grid=(n_head // 4,),
        in_specs=[
            pl.BlockSpec((ROWS, 4 * cols // n_head), lambda i: (0, i)),
            pl.BlockSpec((ROWS, 2 * N), lambda i: (0, i)),
            pl.BlockSpec((ROWS, 2 * N), lambda i: (0, i)),
            pl.BlockSpec((ROWS, ROWS), lambda i: (0, i // 2)),
        ],
        out_specs=[pl.BlockSpec((4,) + shape, lambda i: (i, 0, 0)) for shape in shapes],
        out_shape=[jax.ShapeDtypeStruct((n_head,) + shape, BF16) for shape in shapes],
    )(tokens, b_proj, c_proj, log_decay)


def b_rows(ref):
    pieces = []
    for k in range(ref.shape[0]):
        pieces += [ref[k, :, :N], ref[k, :, N:]]
    return jnp.concatenate(pieces, axis=0)


def c_rows(ref, more_ref):
    pieces = []
    for k in range(ref.shape[0]):
        rest = jnp.concatenate([more_ref[k, :, :LANES], more_ref[k, :, LANES:N]], axis=0)
        pieces += [ref[k, :, :N], jnp.concatenate([ref[k, :, N:], rest], axis=1)]
    return jnp.concatenate(pieces, axis=0)


def rows_of(ref):
    return jnp.concatenate([ref[k] for k in range(ref.shape[0])], axis=0)


def three(whole):
    high = whole.astype(BF16).astype(F32)
    mid = (whole - high).astype(BF16).astype(F32)
    return high, mid, whole - high - mid


def in_pieces(whole):
    high, mid, low = three(whole)
    row = lax.broadcasted_iota(jnp.int32, (PIECES, whole.shape[1]), 0)
    out = jnp.where(row == 0, high, jnp.where(row == 1, mid, jnp.where(row == 2, low, 0.0)))
    return out.astype(BF16)


def of_pieces(rows):
    return jnp.sum(rows.astype(F32), axis=0, keepdims=True)


def block_sums(d_ref, block):
    turned = jnp.concatenate([d_ref[2 * block], d_ref[2 * block + 1]], axis=1)
    u = lax.broadcasted_iota(jnp.int32, (Q, Q), 0)
    t = lax.broadcasted_iota(jnp.int32, (Q, Q), 1)
    upper = (u <= t).astype(F32).astype(BF16)
    sums = dot(turned, upper, ((1,), (0,))) * LOG2E
    rest = jnp.zeros((LANES - 3 * HEADS, Q), F32)
    return jnp.transpose(jnp.concatenate([*three(sums), rest], axis=0)).astype(BF16)


def spread_sums(part, pieces, width):
    row = lax.broadcasted_iota(jnp.int32, (LANES, width), 0)
    col = lax.broadcasted_iota(jnp.int32, (LANES, width), 1)
    head = col // P_SIZE + first_head(part)
    taken = jnp.logical_and(row % HEADS == head, row < 3 * HEADS)
    return dot(pieces, taken.astype(F32).astype(BF16), ((1,), (0,)))


def step_of(i, shift):
    return jnp.maximum(i - shift, 0)


def x_spec(width, shift=0):
    return pl.BlockSpec((SLABS, ROWS, width), lambda i: (step_of(i, shift), 0, 0))


def b_spec(shift=0):
    return pl.BlockSpec((SLABS, HALF, 2 * N), lambda i: (step_of(i, shift), ROWS // HALF, 0))


def c_specs(shift=0):
    width = PART_HEADS[1] * P_SIZE
    return [
        pl.BlockSpec((SLABS, HALF, width), lambda i: (step_of(i, shift), ROWS // HALF, 0)),
        pl.BlockSpec(
            (SLABS, HALF // 2, width),
            lambda i: (step_of(i, shift), 2 * (ROWS + HALF) // HALF, 0),
        ),
    ]


def flat_spec(width, shift=0):
    return pl.BlockSpec((SLABS * ROWS, width), lambda i: (step_of(i, shift), 0))


def smem_spec():
    return pl.BlockSpec(memory_space=pltpu.SMEM)


BLOCKS = SLABS * ROWS // Q


def states_kernel(part, *refs):
    if part == 0:
        core_ref, x_ref, b_ref, d_ref, keep_ref, send_ref, sums_ref, state, total = refs
    else:
        core_ref, x_ref, b_ref, sums_ref, keep_ref, send_ref, state, total = refs
    step = pl.program_id(0)
    width = x_ref.shape[2]

    @pl.when(step == 0)
    def _():
        state[...] = jnp.zeros_like(state)
        total[...] = jnp.zeros_like(total)

    if part == 0:
        pieces = jnp.concatenate([block_sums(d_ref, k) for k in range(BLOCKS)], axis=0)
        sums_ref[...] = pieces
    else:
        pieces = sums_ref[...]
    s = spread_sums(part, pieces, width)
    later = jnp.zeros((1, width), F32)
    shares = []
    for k in reversed(range(BLOCKS)):
        here = s[k * Q : (k + 1) * Q]
        later = later + here[Q - 1 : Q]
        shares = [jnp.exp2(later - here)] + shares
    xw = (rows_of(x_ref).astype(F32) * jnp.concatenate(shares, axis=0)).astype(BF16)
    state[...] = state[...] * jnp.exp2(later) + dot(b_rows(b_ref), xw, ((0,), (0,)))
    total[...] += later

    @pl.when(step == pl.num_programs(0) - 1)
    def _():
        pieces = in_pieces(total[...])
        top, low = state[: N // 2], state[N // 2 :]
        first = core_ref[0] == 0
        keep_ref[: N // 2] = jnp.where(first, top, low).astype(BF16)
        send_ref[: N // 2] = jnp.where(first, low, top).astype(BF16)
        keep_ref[N // 2 :] = pieces
        send_ref[N // 2 :] = pieces


def end_states(part, core, first, msg, sums=None):
    slabs, _, width = msg.shape
    shape = (N // 2 + PIECES, width)
    d_spec = pl.BlockSpec((SLABS, HEADS, LANES), lambda i: (i, ROWS // HEADS, 2 * N // LANES))
    out_specs = [pl.BlockSpec(shape, lambda i: (0, 0))] * 2
    out_shape = [jax.ShapeDtypeStruct(shape, BF16)] * 2
    if part == 0:
        out_specs.append(flat_spec(LANES))
        out_shape.append(jax.ShapeDtypeStruct((slabs * ROWS, LANES), BF16))
    return call(
        functools.partial(states_kernel, part),
        "states%d" % part,
        (2**30, 5, 2**20),
        limit=(60 - 20 * part) * 1024 * 1024,
        grid=(slabs // SLABS,),
        in_specs=[
            smem_spec(),
            x_spec(width),
            b_spec(),
            d_spec if part == 0 else flat_spec(LANES),
        ],
        out_specs=out_specs,
        out_shape=out_shape,
        scratch_shapes=[pltpu.VMEM((N, width), F32), pltpu.VMEM((1, width), F32)],
    )(core, msg, *far(first, first if part == 0 else sums))


def halves(core_ref, keep_ref, got_ref):
    first = core_ref[0] == 0
    keep, got = keep_ref[...].astype(F32), got_ref[...].astype(F32)
    early, late = jnp.where(first, keep, got), jnp.where(first, got, keep)
    rows = N // 2
    return early[:rows], of_pieces(early[rows:]), late[:rows], of_pieces(late[rows:])


def chip_kernel(core_ref, keep_ref, got_ref, out_ref):
    early, early_total, late, late_total = halves(core_ref, keep_ref, got_ref)
    out_ref[: N // 2] = (early * jnp.exp2(late_total) + late).astype(BF16)
    out_ref[N // 2 :] = in_pieces(early_total + late_total)


def chip_state(part, core, keep, got):
    return call(
        chip_kernel,
        "chip%d" % part,
        (2**18, 1, 0),
        limit=16 * 1024 * 1024,
        in_specs=[smem_spec()] + [pl.BlockSpec(memory_space=pltpu.VMEM)] * 2,
        out_specs=pl.BlockSpec(memory_space=pltpu.VMEM),
        out_shape=jax.ShapeDtypeStruct(keep.shape, BF16),
    )(core, keep, got)


def start_kernel(core_ref, chip_ref, keep_ref, got_ref, *refs):
    mine_ref, theirs_ref, state = refs[-3:]
    others = refs[:-3]
    state[...] = jnp.zeros_like(state)
    for k in reversed(range(len(others))):

        @pl.when(k + 1 <= chip_ref[0])
        def _():
            ref = others[k]
            state[...] = state[...] * jnp.exp2(of_pieces(ref[N // 2 :])) + ref[: N // 2].astype(F32)

    early, early_total, _, _ = halves(core_ref, keep_ref, got_ref)
    before = state[...]
    after = before * jnp.exp2(early_total) + early
    first = core_ref[0] == 0
    mine_ref[...] = jnp.where(first, before, after).astype(BF16)
    theirs_ref[...] = jnp.where(first, after, before).astype(BF16)


def start_state(part, core, chip, keep, got, others):
    shape = (N // 2, keep.shape[1])
    vmem = pl.BlockSpec(memory_space=pltpu.VMEM)
    return call(
        start_kernel,
        "start%d" % part,
        (2**20, 2, 0),
        limit=16 * 1024 * 1024,
        in_specs=[smem_spec()] * 2 + [vmem] * (2 + len(others)),
        out_specs=[vmem] * 2,
        out_shape=[jax.ShapeDtypeStruct(shape, BF16)] * 2,
        scratch_shapes=[pltpu.VMEM(shape, F32)],
    )(core, chip, keep, got, *others)


def incoming(part, core, chip, keep, send, beside=None):
    shards = lax.axis_size("ctx")
    swap = [(i, i ^ 1) for i in range(shards)]
    ahead = [(i, (i + CORES) % shards) for i in range(shards)]
    back = [(i, (i - CORES) % shards) for i in range(shards)]
    got = lax.ppermute(send, "ctx", swap)
    own = chip_state(part, core, keep, got)
    chips = shards // CORES
    forward, backward = [own], [own]
    for step in range(chips // 2):
        forward.append(lax.ppermute(forward[-1], "ctx", ahead))
        if step < chips - 1 - chips // 2:
            backward.append(lax.ppermute(backward[-1], "ctx", back))
        if step == 0 and beside is not None:
            forward[-1], backward[-1], beside = lax.optimization_barrier(
                (forward[-1], backward[-1], beside)
            )
    mine, theirs = start_state(part, core, chip, keep, got, forward[1:] + backward[:0:-1])
    return mine, lax.ppermute(theirs, "ctx", swap), beside


def gain_row(part, gain_ref, width):
    head = lax.broadcasted_iota(jnp.int32, (1, width), 1) // P_SIZE
    row = jnp.zeros((1, width), F32)
    for h in range(PART_HEADS[part]):
        row = jnp.where(head == h, gain_ref[first_head(part) + h], row)
    return row


def own_tokens(part, x_ref, b_ref, c_refs, sums_ref, gain_ref, state, write):
    width = x_ref.shape[2]
    t = lax.broadcasted_iota(jnp.int32, (Q, Q), 0)
    u = lax.broadcasted_iota(jnp.int32, (Q, Q), 1)
    gain = gain_row(part, gain_ref, width)
    x_all = rows_of(x_ref).astype(F32)
    b_all = b_rows(b_ref)
    c_all = c_rows(*c_refs)
    s_all = spread_sums(part, sums_ref[...], width)
    for k in range(BLOCKS):
        block = slice(k * Q, (k + 1) * Q)
        xf, b, c, s = x_all[block], b_all[block], c_all[block], s_all[block]
        end = s[Q - 1 : Q]
        scores = jnp.where(t >= u, dot(c, b, ((1,), (1,))), 0.0).astype(BF16)
        before = state[...]
        rest = dot(c, before.astype(BF16), ((1,), (0,))) * jnp.exp2(s) + gain * xf
        state[...] = before * jnp.exp2(end) + dot(
            b, (xf * jnp.exp2(end - s)).astype(BF16), ((0,), (0,))
        )
        for i in range(Q // SUB):
            here = slice(i * SUB, (i + 1) * SUB)
            upto = (i + 1) * SUB
            mid = s[i * SUB + SUB // 2 - 1 : i * SUB + SUB // 2]
            xw = (xf[:upto] * jnp.exp2(mid - s[:upto])).astype(BF16)
            inner = dot(scores[here, :upto], xw, ((1,), (0,))) * jnp.exp2(s[here] - mid)
            write(k * Q + i * SUB, inner + rest[here])


def start_from(core_ref, mine_ref, got_ref, state):
    @pl.when(pl.program_id(0) == 0)
    def _():
        first = core_ref[0] == 0
        mine, got = mine_ref[...].astype(F32), got_ref[...].astype(F32)
        state[: N // 2] = jnp.where(first, mine, got).astype(state.dtype)
        state[N // 2 :] = jnp.where(first, got, mine).astype(state.dtype)


def half_spec(width):
    return pl.BlockSpec((N // 2, width), lambda i: (0, 0))


def mix_kernel(
    part, core_ref, gain_ref, mine_ref, got_ref, x_ref, b_ref, c_ref, more_ref, sums_ref, out_ref, state
):
    start_from(core_ref, mine_ref, got_ref, state)

    def write(at, rows):
        out_ref[at // ROWS, at % ROWS : at % ROWS + rows.shape[0]] = rows.astype(BF16)

    own_tokens(part, x_ref, b_ref, (c_ref, more_ref), sums_ref, gain_ref, state, write)


def mix(part, core, mine, got, first, second, sums, gains):
    slabs, _, width = (first, second)[part].shape
    return call(
        functools.partial(mix_kernel, part),
        "mix%d" % part,
        (4 * 2**30, 14, 2**22),
        limit=44 * 1024 * 1024,
        grid=(slabs // SLABS,),
        in_specs=[smem_spec()] * 2
        + [half_spec(width)] * 2
        + [x_spec(width), b_spec(), *c_specs(), flat_spec(LANES)],
        out_specs=x_spec(width),
        out_shape=jax.ShapeDtypeStruct((slabs, ROWS, width), BF16),
        scratch_shapes=[pltpu.VMEM((N, width), F32)],
    )(core, gains, mine, got, *far(first, first), second, second, *far(sums))


def inside_kernel(part, gain_ref, x_ref, b_ref, c_ref, more_ref, sums_ref, out_ref, state):
    @pl.when(pl.program_id(0) == 0)
    def _():
        state[...] = jnp.zeros_like(state)

    def write(at, rows):
        out_ref[at : at + rows.shape[0]] = rows.astype(out_ref.dtype)

    own_tokens(part, x_ref, b_ref, (c_ref, more_ref), sums_ref, gain_ref, state, write)


def inside(part, first, second, sums, gains):
    slabs, _, width = (first, second)[part].shape
    return call(
        functools.partial(inside_kernel, part),
        "inside%d" % part,
        (4 * 2**30, 14, 2**22),
        grid=(slabs // SLABS,),
        in_specs=[
            smem_spec(),
            x_spec(width),
            b_spec(),
            *c_specs(),
            flat_spec(LANES),
        ],
        out_specs=flat_spec(width),
        out_shape=jax.ShapeDtypeStruct((slabs * ROWS, width), BF16),
        scratch_shapes=[pltpu.VMEM((N, width), F32)],
    )(gains, *far((first, second)[part], first, second, second, sums))


def join_kernel(
    part, core_ref, mine_ref, got_ref, c_ref, more_ref, sums_ref, own_ref, out_ref, start, total
):
    width = own_ref.shape[1]
    start_from(core_ref, mine_ref, got_ref, start)

    @pl.when(pl.program_id(0) == 0)
    def _():
        total[...] = jnp.zeros_like(total)

    s = spread_sums(part, sums_ref[...], width)
    outer = dot(c_rows(c_ref, more_ref), start[...], ((1,), (0,)))
    since = total[...]
    for k in range(BLOCKS):
        here = s[k * Q : (k + 1) * Q]
        for j in range(Q // ROWS):
            some = slice(j * ROWS, (j + 1) * ROWS)
            at = slice(k * Q + j * ROWS, k * Q + (j + 1) * ROWS)
            out_ref[at.start // ROWS] = (
                own_ref[at].astype(F32) + outer[at] * jnp.exp2(here[some] + since)
            ).astype(BF16)
        since = since + here[Q - 1 : Q]
    total[...] = since


def join(part, core, mine, got, first, second, sums, own):
    slabs, _, width = (first, second)[part].shape
    return call(
        functools.partial(join_kernel, part),
        "join%d" % part,
        (2**30, 8, 2**20),
        grid=(slabs // SLABS,),
        in_specs=[smem_spec()]
        + [half_spec(width)] * 2
        + [*c_specs(), flat_spec(LANES), flat_spec(width)],
        out_specs=x_spec(width),
        out_shape=jax.ShapeDtypeStruct((slabs, ROWS, width), BF16),
        scratch_shapes=[pltpu.VMEM((N, width), BF16), pltpu.VMEM((1, width), F32)],
    )(core, mine, got, *far(second, second, sums, own))


def unpack_kernel(part, *refs):
    y_ref, out_ref, sems = refs[0], refs[-2], refs[-1]
    width = y_ref.shape[2]
    copies = []
    for k in range(y_ref.shape[0]):
        at = (k * HEADS + first_head(part)) * P_SIZE
        copies.append(
            pltpu.make_async_copy(y_ref.at[k], out_ref.at[:, at : at + width], sems.at[k])
        )
    for copy in copies:
        copy.start()
    for copy in copies:
        copy.wait()


def unpack(part, y, before=()):
    n_head, rows, width = y.shape
    return call(
        functools.partial(unpack_kernel, part),
        "unpack%d" % part,
        (0, 4, 0),
        limit=16 * 1024 * 1024,
        in_specs=[pl.BlockSpec(memory_space=pltpu.VMEM)]
        + [pl.BlockSpec(memory_space=pl.ANY)] * len(before),
        out_specs=pl.BlockSpec(memory_space=pl.ANY),
        out_shape=jax.ShapeDtypeStruct((rows, n_head * HEADS * P_SIZE), BF16),
        scratch_shapes=[pltpu.SemaphoreType.DMA((n_head,))],
        input_output_aliases={1: 0} if before else {},
    )(y, *before)


def exchange(msg):
    return lax.all_to_all(msg, "head", split_axis=0, concat_axis=0, tiled=True)


def local(tokens, b_proj, c_proj, log_decay, bypass_gain_vector):
    n_head = lax.axis_size("head")
    me = lax.axis_index("ctx").astype(jnp.int32).reshape(1)
    core, chip = me % CORES, me // CORES
    gains = bypass_gain_vector
    after = lax.optimization_barrier
    packed0, packed1 = pack(tokens, b_proj, c_proj, log_decay, n_head)
    first = exchange(packed0)
    packed1, first = after((packed1, first))
    second = exchange(packed1)
    keep0, send0, sums = end_states(0, core, first, first)
    mine0, got0, _ = incoming(0, core, chip, keep0, send0)
    keep1, send1 = end_states(1, core, first, second, sums)
    mine0, send1 = after((mine0, send1))
    mixed0 = mix(0, core, mine0, got0, first, second, sums, gains)
    y0 = exchange(mixed0)

    own1 = inside(1, first, second, sums, gains)
    mine1, got1, own1 = incoming(1, core, chip, keep1, send1, own1)
    mixed1 = join(1, core, mine1, got1, first, second, sums, own1)
    mixed1, y0 = after((mixed1, y0))
    out = unpack(0, y0)
    return unpack(1, exchange(mixed1), (out,))


def solution(mesh):
    rows = P(("ctx", "head"), None)
    return jax.shard_map(
        local,
        mesh=mesh,
        in_specs=(rows, rows, rows, rows, P("head")),
        out_specs=rows,
        check_vma=False,
    )
```

```python
import functools

import jax
import jax.numpy as jnp
from jax import lax
from jax.experimental import pallas as pl
from jax.experimental.pallas import tpu as pltpu
from jax.sharding import PartitionSpec as P

P_SIZE = 64
N = 256
Q = 256
SUB = 64
PART_HEADS = (10, 6)
ROWS = 128
HALF = ROWS // 2
HEADS = 16
SLABS = 4
LANES = 128
PIECES = 16
CORES = 2
LOG2E = 1.4426950408889634
F32 = jnp.float32
BF16 = jnp.bfloat16
VMEM_LIMIT = 60 * 1024 * 1024


def far(*arrays):
    return [pltpu.with_memory_space_constraint(x, pltpu.HBM) for x in arrays]


def dot(a, b, dims):
    return lax.dot_general(a, b, (dims, ((), ())), preferred_element_type=F32)


def call(kernel, name, cost, limit=VMEM_LIMIT, **kwargs):
    flops, mib, exps = cost
    return pl.pallas_call(
        kernel,
        name=name,
        compiler_params=pltpu.CompilerParams(vmem_limit_bytes=limit),
        cost_estimate=pl.CostEstimate(
            flops=flops, bytes_accessed=mib * 2**20, transcendentals=exps
        ),
        **kwargs,
    )


def first_head(part):
    return sum(PART_HEADS[:part])


def pack_kernel(x_ref, b_ref, c_ref, d_ref, first_ref, second_ref):
    dests, _, wide = first_ref.shape
    narrow = second_ref.shape[2]
    turned = jnp.transpose(d_ref[...].astype(F32)).astype(BF16)
    turned = jnp.where(pl.program_id(0) % 2 == 0, turned[: 4 * HEADS], turned[4 * HEADS :])
    low, high = slice(0, LANES), slice(LANES, 2 * LANES)
    for k in range(dests):
        cols = slice((k // 2) * N, (k // 2 + 1) * N)
        at = k * (wide + narrow)
        first_ref[k, :ROWS] = x_ref[:, at : at + wide]
        first_ref[k, ROWS:, :N] = b_ref[:HALF, cols]
        first_ref[k, ROWS:, N : 2 * N] = b_ref[HALF:, cols]
        first_ref[k, ROWS : ROWS + HEADS, 2 * N :] = turned[k * HEADS : (k + 1) * HEADS]
        first_ref[k, ROWS + HEADS :, 2 * N :] = jnp.zeros((HALF - HEADS, LANES), BF16)
        second_ref[k, :ROWS] = x_ref[:, at + wide : at + wide + narrow]
        second_ref[k, ROWS : ROWS + HALF, :N] = c_ref[:HALF, cols]
        rest = c_ref[HALF:, cols]
        second_ref[k, ROWS : ROWS + HALF, N:] = rest[:, low]
        second_ref[k, ROWS + HALF :, low] = rest[: HALF // 2, high]
        second_ref[k, ROWS + HALF :, high] = rest[HALF // 2 :, high]
        second_ref[k, ROWS + HALF :, N:] = jnp.zeros((HALF // 2, LANES), BF16)


def pack(tokens, b_proj, c_proj, log_decay, n_head):
    cols = tokens.shape[1]
    widths = [heads * P_SIZE for heads in PART_HEADS]
    heights = (ROWS + HALF, ROWS + HALF + HALF // 2)
    shapes = list(zip(heights, widths))
    return call(
        pack_kernel,
        "pack",
        (0, 12, 0),
        grid=(n_head // 4,),
        in_specs=[
            pl.BlockSpec((ROWS, 4 * cols // n_head), lambda i: (0, i)),
            pl.BlockSpec((ROWS, 2 * N), lambda i: (0, i)),
            pl.BlockSpec((ROWS, 2 * N), lambda i: (0, i)),
            pl.BlockSpec((ROWS, ROWS), lambda i: (0, i // 2)),
        ],
        out_specs=[pl.BlockSpec((4,) + shape, lambda i: (i, 0, 0)) for shape in shapes],
        out_shape=[jax.ShapeDtypeStruct((n_head,) + shape, BF16) for shape in shapes],
    )(tokens, b_proj, c_proj, log_decay)


def b_rows(ref):
    pieces = []
    for k in range(ref.shape[0]):
        pieces += [ref[k, :, :N], ref[k, :, N:]]
    return jnp.concatenate(pieces, axis=0)


def c_rows(ref, more_ref):
    pieces = []
    for k in range(ref.shape[0]):
        rest = jnp.concatenate([more_ref[k, :, :LANES], more_ref[k, :, LANES:N]], axis=0)
        pieces += [ref[k, :, :N], jnp.concatenate([ref[k, :, N:], rest], axis=1)]
    return jnp.concatenate(pieces, axis=0)


def rows_of(ref):
    return jnp.concatenate([ref[k] for k in range(ref.shape[0])], axis=0)


def three(whole):
    high = whole.astype(BF16).astype(F32)
    mid = (whole - high).astype(BF16).astype(F32)
    return high, mid, whole - high - mid


def in_pieces(whole):
    high, mid, low = three(whole)
    row = lax.broadcasted_iota(jnp.int32, (PIECES, whole.shape[1]), 0)
    out = jnp.where(row == 0, high, jnp.where(row == 1, mid, jnp.where(row == 2, low, 0.0)))
    return out.astype(BF16)


def of_pieces(rows):
    return jnp.sum(rows.astype(F32), axis=0, keepdims=True)


def block_sums(d_ref, block):
    turned = jnp.concatenate([d_ref[2 * block], d_ref[2 * block + 1]], axis=1)
    u = lax.broadcasted_iota(jnp.int32, (Q, Q), 0)
    t = lax.broadcasted_iota(jnp.int32, (Q, Q), 1)
    upper = (u <= t).astype(F32).astype(BF16)
    sums = dot(turned, upper, ((1,), (0,))) * LOG2E
    rest = jnp.zeros((LANES - 3 * HEADS, Q), F32)
    return jnp.transpose(jnp.concatenate([*three(sums), rest], axis=0)).astype(BF16)


def spread_sums(part, pieces, width):
    row = lax.broadcasted_iota(jnp.int32, (LANES, width), 0)
    col = lax.broadcasted_iota(jnp.int32, (LANES, width), 1)
    head = col // P_SIZE + first_head(part)
    taken = jnp.logical_and(row % HEADS == head, row < 3 * HEADS)
    return dot(pieces, taken.astype(F32).astype(BF16), ((1,), (0,)))


def step_of(i, shift):
    return jnp.maximum(i - shift, 0)


def x_spec(width, shift=0):
    return pl.BlockSpec((SLABS, ROWS, width), lambda i: (step_of(i, shift), 0, 0))


def b_spec(shift=0):
    return pl.BlockSpec((SLABS, HALF, 2 * N), lambda i: (step_of(i, shift), ROWS // HALF, 0))


def c_specs(shift=0):
    width = PART_HEADS[1] * P_SIZE
    return [
        pl.BlockSpec((SLABS, HALF, width), lambda i: (step_of(i, shift), ROWS // HALF, 0)),
        pl.BlockSpec(
            (SLABS, HALF // 2, width),
            lambda i: (step_of(i, shift), 2 * (ROWS + HALF) // HALF, 0),
        ),
    ]


def flat_spec(width, shift=0):
    return pl.BlockSpec((SLABS * ROWS, width), lambda i: (step_of(i, shift), 0))


def smem_spec():
    return pl.BlockSpec(memory_space=pltpu.SMEM)


BLOCKS = SLABS * ROWS // Q


def states_kernel(part, *refs):
    if part == 0:
        core_ref, x_ref, b_ref, d_ref, keep_ref, send_ref, sums_ref, state, total = refs
    else:
        core_ref, x_ref, b_ref, sums_ref, keep_ref, send_ref, state, total = refs
    step = pl.program_id(0)
    width = x_ref.shape[2]

    @pl.when(step == 0)
    def _():
        state[...] = jnp.zeros_like(state)
        total[...] = jnp.zeros_like(total)

    if part == 0:
        pieces = jnp.concatenate([block_sums(d_ref, k) for k in range(BLOCKS)], axis=0)
        sums_ref[...] = pieces
    else:
        pieces = sums_ref[...]
    s = spread_sums(part, pieces, width)
    later = jnp.zeros((1, width), F32)
    shares = []
    for k in reversed(range(BLOCKS)):
        here = s[k * Q : (k + 1) * Q]
        later = later + here[Q - 1 : Q]
        shares = [jnp.exp2(later - here)] + shares
    xw = (rows_of(x_ref).astype(F32) * jnp.concatenate(shares, axis=0)).astype(BF16)
    state[...] = state[...] * jnp.exp2(later) + dot(b_rows(b_ref), xw, ((0,), (0,)))
    total[...] += later

    @pl.when(step == pl.num_programs(0) - 1)
    def _():
        pieces = in_pieces(total[...])
        top, low = state[: N // 2], state[N // 2 :]
        first = core_ref[0] == 0
        keep_ref[: N // 2] = jnp.where(first, top, low).astype(BF16)
        send_ref[: N // 2] = jnp.where(first, low, top).astype(BF16)
        keep_ref[N // 2 :] = pieces
        send_ref[N // 2 :] = pieces


def end_states(part, core, first, msg, sums=None):
    slabs, _, width = msg.shape
    shape = (N // 2 + PIECES, width)
    d_spec = pl.BlockSpec((SLABS, HEADS, LANES), lambda i: (i, ROWS // HEADS, 2 * N // LANES))
    out_specs = [pl.BlockSpec(shape, lambda i: (0, 0))] * 2
    out_shape = [jax.ShapeDtypeStruct(shape, BF16)] * 2
    if part == 0:
        out_shape[0] = pltpu.VMEM(shape, BF16)
    if part == 0:
        out_specs.append(flat_spec(LANES))
        out_shape.append(jax.ShapeDtypeStruct((slabs * ROWS, LANES), BF16))
    return call(
        functools.partial(states_kernel, part),
        "states%d" % part,
        (2**30, 5, 2**20),
        limit=(60 - 20 * part) * 1024 * 1024,
        grid=(slabs // SLABS,),
        in_specs=[
            smem_spec(),
            x_spec(width),
            b_spec(),
            d_spec if part == 0 else flat_spec(LANES),
        ],
        out_specs=out_specs,
        out_shape=out_shape,
        scratch_shapes=[pltpu.VMEM((N, width), F32), pltpu.VMEM((1, width), F32)],
    )(core, msg, *far(first, first if part == 0 else sums))


def halves(core_ref, keep_ref, got_ref):
    first = core_ref[0] == 0
    keep, got = keep_ref[...].astype(F32), got_ref[...].astype(F32)
    early, late = jnp.where(first, keep, got), jnp.where(first, got, keep)
    rows = N // 2
    return early[:rows], of_pieces(early[rows:]), late[:rows], of_pieces(late[rows:])


def chip_kernel(core_ref, keep_ref, got_ref, out_ref):
    early, early_total, late, late_total = halves(core_ref, keep_ref, got_ref)
    out_ref[: N // 2] = (early * jnp.exp2(late_total) + late).astype(BF16)
    out_ref[N // 2 :] = in_pieces(early_total + late_total)


def chip_state(part, core, keep, got):
    return call(
        chip_kernel,
        "chip%d" % part,
        (2**18, 1, 0),
        limit=16 * 1024 * 1024,
        in_specs=[smem_spec()] + [pl.BlockSpec(memory_space=pltpu.VMEM)] * 2,
        out_specs=pl.BlockSpec(memory_space=pltpu.VMEM),
        out_shape=jax.ShapeDtypeStruct(keep.shape, BF16),
    )(core, keep, got)


def start_kernel(core_ref, chip_ref, keep_ref, got_ref, *refs):
    mine_ref, theirs_ref, state = refs[-3:]
    others = refs[:-3]
    state[...] = jnp.zeros_like(state)
    for k in reversed(range(len(others))):

        @pl.when(k + 1 <= chip_ref[0])
        def _():
            ref = others[k]
            state[...] = state[...] * jnp.exp2(of_pieces(ref[N // 2 :])) + ref[: N // 2].astype(F32)

    early, early_total, _, _ = halves(core_ref, keep_ref, got_ref)
    before = state[...]
    after = before * jnp.exp2(early_total) + early
    first = core_ref[0] == 0
    mine_ref[...] = jnp.where(first, before, after).astype(BF16)
    theirs_ref[...] = jnp.where(first, after, before).astype(BF16)


def start_state(part, core, chip, keep, got, others):
    shape = (N // 2, keep.shape[1])
    vmem = pl.BlockSpec(memory_space=pltpu.VMEM)
    return call(
        start_kernel,
        "start%d" % part,
        (2**20, 2, 0),
        limit=16 * 1024 * 1024,
        in_specs=[smem_spec()] * 2 + [vmem] * (2 + len(others)),
        out_specs=[vmem] * 2,
        out_shape=[jax.ShapeDtypeStruct(shape, BF16)] * 2,
        scratch_shapes=[pltpu.VMEM(shape, F32)],
    )(core, chip, keep, got, *others)


def incoming(part, core, chip, keep, send, beside=None):
    shards = lax.axis_size("ctx")
    swap = [(i, i ^ 1) for i in range(shards)]
    ahead = [(i, (i + CORES) % shards) for i in range(shards)]
    back = [(i, (i - CORES) % shards) for i in range(shards)]
    got = lax.ppermute(send, "ctx", swap)
    own = chip_state(part, core, keep, got)
    chips = shards // CORES
    forward, backward = [own], [own]
    for step in range(chips // 2):
        forward.append(lax.ppermute(forward[-1], "ctx", ahead))
        if step < chips - 1 - chips // 2:
            backward.append(lax.ppermute(backward[-1], "ctx", back))
        if step == 0 and beside is not None:
            forward[-1], backward[-1], beside = lax.optimization_barrier(
                (forward[-1], backward[-1], beside)
            )
    mine, theirs = start_state(part, core, chip, keep, got, forward[1:] + backward[:0:-1])
    return mine, lax.ppermute(theirs, "ctx", swap), beside


def gain_row(part, gain_ref, width):
    head = lax.broadcasted_iota(jnp.int32, (1, width), 1) // P_SIZE
    row = jnp.zeros((1, width), F32)
    for h in range(PART_HEADS[part]):
        row = jnp.where(head == h, gain_ref[first_head(part) + h], row)
    return row


def own_tokens(part, x_ref, b_ref, c_refs, sums_ref, gain_ref, state, write):
    width = x_ref.shape[2]
    t = lax.broadcasted_iota(jnp.int32, (Q, Q), 0)
    u = lax.broadcasted_iota(jnp.int32, (Q, Q), 1)
    gain = gain_row(part, gain_ref, width)
    x_all = rows_of(x_ref).astype(F32)
    b_all = b_rows(b_ref)
    c_all = c_rows(*c_refs)
    s_all = spread_sums(part, sums_ref[...], width)
    for k in range(BLOCKS):
        block = slice(k * Q, (k + 1) * Q)
        xf, b, c, s = x_all[block], b_all[block], c_all[block], s_all[block]
        end = s[Q - 1 : Q]
        scores = jnp.where(t >= u, dot(c, b, ((1,), (1,))), 0.0).astype(BF16)
        before = state[...]
        rest = dot(c, before.astype(BF16), ((1,), (0,))) * jnp.exp2(s) + gain * xf
        state[...] = before * jnp.exp2(end) + dot(
            b, (xf * jnp.exp2(end - s)).astype(BF16), ((0,), (0,))
        )
        for i in range(Q // SUB):
            here = slice(i * SUB, (i + 1) * SUB)
            upto = (i + 1) * SUB
            mid = s[i * SUB + SUB // 2 - 1 : i * SUB + SUB // 2]
            xw = (xf[:upto] * jnp.exp2(mid - s[:upto])).astype(BF16)
            inner = dot(scores[here, :upto], xw, ((1,), (0,))) * jnp.exp2(s[here] - mid)
            write(k * Q + i * SUB, inner + rest[here])


def start_from(core_ref, mine_ref, got_ref, state):
    @pl.when(pl.program_id(0) == 0)
    def _():
        first = core_ref[0] == 0
        mine, got = mine_ref[...].astype(F32), got_ref[...].astype(F32)
        state[: N // 2] = jnp.where(first, mine, got).astype(state.dtype)
        state[N // 2 :] = jnp.where(first, got, mine).astype(state.dtype)


def half_spec(width):
    return pl.BlockSpec((N // 2, width), lambda i: (0, 0))


def mix_kernel(
    part, core_ref, gain_ref, mine_ref, got_ref, x_ref, b_ref, c_ref, more_ref, sums_ref, out_ref, state
):
    start_from(core_ref, mine_ref, got_ref, state)

    def write(at, rows):
        out_ref[at // ROWS, at % ROWS : at % ROWS + rows.shape[0]] = rows.astype(BF16)

    own_tokens(part, x_ref, b_ref, (c_ref, more_ref), sums_ref, gain_ref, state, write)


def mix(part, core, mine, got, first, second, sums, gains):
    slabs, _, width = (first, second)[part].shape
    return call(
        functools.partial(mix_kernel, part),
        "mix%d" % part,
        (4 * 2**30, 14, 2**22),
        limit=44 * 1024 * 1024,
        grid=(slabs // SLABS,),
        in_specs=[smem_spec()] * 2
        + [half_spec(width)] * 2
        + [x_spec(width), b_spec(), *c_specs(), flat_spec(LANES)],
        out_specs=x_spec(width),
        out_shape=jax.ShapeDtypeStruct((slabs, ROWS, width), BF16),
        scratch_shapes=[pltpu.VMEM((N, width), F32)],
    )(core, gains, mine, got, *far(first, first), second, second, *far(sums))


def inside_kernel(part, gain_ref, x_ref, b_ref, c_ref, more_ref, sums_ref, out_ref, state):
    @pl.when(pl.program_id(0) == 0)
    def _():
        state[...] = jnp.zeros_like(state)

    def write(at, rows):
        out_ref[at : at + rows.shape[0]] = rows.astype(out_ref.dtype)

    own_tokens(part, x_ref, b_ref, (c_ref, more_ref), sums_ref, gain_ref, state, write)


def inside(part, first, second, sums, gains):
    slabs, _, width = (first, second)[part].shape
    return call(
        functools.partial(inside_kernel, part),
        "inside%d" % part,
        (4 * 2**30, 14, 2**22),
        grid=(slabs // SLABS,),
        in_specs=[
            smem_spec(),
            x_spec(width),
            b_spec(),
            *c_specs(),
            flat_spec(LANES),
        ],
        out_specs=flat_spec(width),
        out_shape=jax.ShapeDtypeStruct((slabs * ROWS, width), BF16),
        scratch_shapes=[pltpu.VMEM((N, width), F32)],
    )(gains, *far((first, second)[part], first, second, second, sums))


def join_kernel(
    part, core_ref, mine_ref, got_ref, c_ref, more_ref, sums_ref, own_ref, out_ref, start, total
):
    width = own_ref.shape[1]
    start_from(core_ref, mine_ref, got_ref, start)

    @pl.when(pl.program_id(0) == 0)
    def _():
        total[...] = jnp.zeros_like(total)

    s = spread_sums(part, sums_ref[...], width)
    outer = dot(c_rows(c_ref, more_ref), start[...], ((1,), (0,)))
    since = total[...]
    for k in range(BLOCKS):
        here = s[k * Q : (k + 1) * Q]
        for j in range(Q // ROWS):
            some = slice(j * ROWS, (j + 1) * ROWS)
            at = slice(k * Q + j * ROWS, k * Q + (j + 1) * ROWS)
            out_ref[at.start // ROWS] = (
                own_ref[at].astype(F32) + outer[at] * jnp.exp2(here[some] + since)
            ).astype(BF16)
        since = since + here[Q - 1 : Q]
    total[...] = since


def join(part, core, mine, got, first, second, sums, own):
    slabs, _, width = (first, second)[part].shape
    return call(
        functools.partial(join_kernel, part),
        "join%d" % part,
        (2**30, 8, 2**20),
        limit=44 * 1024 * 1024,
        grid=(slabs // SLABS,),
        in_specs=[smem_spec()]
        + [half_spec(width)] * 2
        + [*c_specs(), flat_spec(LANES), flat_spec(width)],
        out_specs=x_spec(width),
        out_shape=pltpu.HBM((slabs, ROWS, width), BF16),
        scratch_shapes=[pltpu.VMEM((N, width), BF16), pltpu.VMEM((1, width), F32)],
    )(core, mine, got, *far(second, second, sums, own))


def unpack_kernel(part, *refs):
    y_ref, out_ref, sems = refs[0], refs[-2], refs[-1]
    width = y_ref.shape[2]
    copies = []
    for k in range(y_ref.shape[0]):
        at = (k * HEADS + first_head(part)) * P_SIZE
        copies.append(
            pltpu.make_async_copy(y_ref.at[k], out_ref.at[:, at : at + width], sems.at[k])
        )
    for copy in copies:
        copy.start()
    for copy in copies:
        copy.wait()


def unpack(part, y, before=()):
    n_head, rows, width = y.shape
    return call(
        functools.partial(unpack_kernel, part),
        "unpack%d" % part,
        (0, 4, 0),
        limit=16 * 1024 * 1024,
        in_specs=[pl.BlockSpec(memory_space=pltpu.VMEM)]
        + [pl.BlockSpec(memory_space=pl.ANY)] * len(before),
        out_specs=pl.BlockSpec(memory_space=pl.ANY),
        out_shape=jax.ShapeDtypeStruct((rows, n_head * HEADS * P_SIZE), BF16),
        scratch_shapes=[pltpu.SemaphoreType.DMA((n_head,))],
        input_output_aliases={1: 0} if before else {},
    )(y, *before)


def exchange(msg):
    return lax.all_to_all(msg, "head", split_axis=0, concat_axis=0, tiled=True)


def local(tokens, b_proj, c_proj, log_decay, bypass_gain_vector):
    n_head = lax.axis_size("head")
    me = lax.axis_index("ctx").astype(jnp.int32).reshape(1)
    core, chip = me % CORES, me // CORES
    gains = bypass_gain_vector
    after = lax.optimization_barrier
    packed0, packed1 = pack(tokens, b_proj, c_proj, log_decay, n_head)
    first = exchange(packed0)
    packed1, first = after((packed1, first))
    second = exchange(packed1)
    keep0, send0, sums = end_states(0, core, first, first)
    mine0, got0, _ = incoming(0, core, chip, keep0, send0)
    keep1, send1 = end_states(1, core, first, second, sums)
    mine0, send1 = after((mine0, send1))
    mixed0 = mix(0, core, mine0, got0, first, second, sums, gains)
    y0 = exchange(mixed0)

    own1 = inside(1, first, second, sums, gains)
    mine1, got1, own1 = incoming(1, core, chip, keep1, send1, own1)
    mixed1 = join(1, core, mine1, got1, first, second, sums, own1)
    mixed1, y0 = after((mixed1, y0))
    out = unpack(0, y0)
    return unpack(1, exchange(mixed1), (out,))


def solution(mesh):
    rows = P(("ctx", "head"), None)
    return jax.shard_map(
        local,
        mesh=mesh,
        in_specs=(rows, rows, rows, rows, P("head")),
        out_specs=rows,
        check_vma=False,
    )
```
